256 devices in a mesh: head: 4 (over x_hi, core), outer: 16 (over x_lo, z), inner: 4 (over y).
Axes of the slice: x: 4 (x_hi: 2, x_lo: 2; x = x_hi * 2 + x_lo), y: 4, z: 8, core: 2. Of those that a mesh axis runs over, the one named last changes fastest.
Arguments:
- queries: bfloat16 [8192, 2048], P(('head', 'outer', 'inner')), may hold values from -5 to 5
- keys: bfloat16 [8192, 512], P(('head', 'outer', 'inner')), may hold values from -5 to 5
- values: bfloat16 [8192, 512], P(('head', 'outer', 'inner')), may hold values from -6 to 6
- grad_out: bfloat16 [8192, 2048], P(('head', 'outer', 'inner')), may hold values from -6 to 6
- block_order: int32 [256], replicated, may hold values from 0 to 255, each once
Outputs:
- attended: bfloat16 [8192, 2048], P(('head', 'outer', 'inner'))
- grad_queries: bfloat16 [8192, 2048], P(('head', 'outer', 'inner'))
- key_gradient: bfloat16 [8192, 512], P(('head', 'outer', 'inner'))
- value_gradient: bfloat16 [8192, 512], P(('head', 'outer', 'inner'))
The draws below stay inside these ranges and needn't reach their ends.
All inputs are finite; a program needn't handle non-finite values.
Results may differ from the reference program's by a relative error of at most 0.028.
Values may be sent and summed in bfloat16 or wider, within the bound.
No kernel may reach another device: no remote copies, remote signals or barrier semaphores. Data moves between devices by JAX's collectives and lax.ppermute only.
A program may use at most 128 MiB of HBM per device.

```python
import math
import jax
import jax.numpy as jnp
from jax import lax

QUERY_HEAD_COUNT = 16
KEY_VALUE_HEADS = 4
HEAD_WIDTH = 128
TOKEN_COUNT = 8192
BLK = 32
NBLK = 256


def draw_queries(key, part):
    key = jax.random.fold_in(key, 1)
    return jnp.clip(jax.random.normal(key, (TOKEN_COUNT, QUERY_HEAD_COUNT * HEAD_WIDTH), jnp.float32), -4.8, 4.8).astype(jnp.bfloat16)


def draw_keys(key, part):
    key = jax.random.fold_in(key, 2)
    return jnp.clip(jax.random.normal(key, (TOKEN_COUNT, KEY_VALUE_HEADS * HEAD_WIDTH), jnp.float32), -4.8, 4.8).astype(jnp.bfloat16)


def block_scale(own_key, dims, cuts, least, top_value):
    gain, own = 1.0, jax.random.fold_in(own_key, 6)
    for dim, parts in cuts:
        draws = jnp.exp(jax.random.uniform(jax.random.fold_in(own, dim), (parts,), jnp.float32, least / len(cuts), top_value / len(cuts)))
        gain = gain * jnp.repeat(draws, dims[dim] // parts).reshape([-1 if axis == dim else 1 for axis in range(len(dims))])
    return gain


def bell_draw(stream_key, shape, width, limit, shards=(), kind=jnp.bfloat16):
    loudness = block_scale(stream_key, shape, shards, -0.22, 0.18) if shards else 1.0
    drawn = jax.random.normal(stream_key, shape, jnp.float32) * width * loudness
    return jnp.minimum(jnp.maximum(drawn, -limit), limit).astype(kind)


def setup_inputs(seed: int = 0) -> dict:
    seeds = jax.random.split(jax.random.key(seed), 6)
    queries = draw_queries(jax.random.fold_in(seeds[5], 71), 0)
    keys = draw_keys(jax.random.fold_in(seeds[5], 71), 0)
    values = bell_draw(seeds[2], (TOKEN_COUNT, KEY_VALUE_HEADS * HEAD_WIDTH), 1.0, 6.0, ((0, 256),))
    grad_out = bell_draw(seeds[3], (TOKEN_COUNT, QUERY_HEAD_COUNT * HEAD_WIDTH), 1.0, 6.0, ((0, 256),))
    block_order = jax.random.permutation(seeds[4], NBLK).astype(jnp.int32)
    return {"queries": queries, "keys": keys, "values": values, "grad_out": grad_out, "block_order": block_order}


def stored_positions(block_order):
    rows = jnp.arange(TOKEN_COUNT, dtype=jnp.int32)
    return block_order[rows // BLK] * BLK + rows % BLK

def head_pass(query_head, key_head, value_head, grad_head, positions):
    score_scale = 1.0 / math.sqrt(HEAD_WIDTH)
    size = math.gcd(TOKEN_COUNT, 512)

    def one_block(carried, block_index):
        key_partial_sum, value_partial_sum = carried
        first = block_index * size
        query_rows = lax.dynamic_slice_in_dim(query_head, first, size, 0)
        grad_rows = lax.dynamic_slice_in_dim(grad_head, first, size, 0)
        query_pos = lax.dynamic_slice_in_dim(positions, first, size, 0)
        allowed = positions[None, :] <= query_pos[:, None]
        scores = jnp.dot(query_rows, key_head.T, preferred_element_type=jnp.float32) * score_scale
        masked = jnp.where(allowed, scores, -jnp.inf)
        row_max = lax.optimization_barrier(jnp.max(masked, axis=1, keepdims=True))
        weights = jnp.where(allowed, jnp.exp(masked - row_max), 0.0)
        totals = lax.optimization_barrier(jnp.sum(weights, axis=1, keepdims=True))
        attended = (jnp.dot(weights.astype(jnp.bfloat16), value_head, preferred_element_type=jnp.float32) / totals).astype(jnp.bfloat16)
        log_total = row_max + jnp.log(totals)
        row_delta = lax.optimization_barrier(jnp.sum(grad_rows.astype(jnp.float32) * attended.astype(jnp.float32), axis=1, keepdims=True))
        probs = jnp.where(allowed, jnp.exp(masked - log_total), 0.0)
        grad_probs = jnp.dot(grad_rows, value_head.T, preferred_element_type=jnp.float32)
        grad_scores = (probs * (grad_probs - row_delta)).astype(jnp.bfloat16)
        grad_query = (jnp.dot(grad_scores, key_head, preferred_element_type=jnp.float32) * score_scale).astype(jnp.bfloat16)
        key_partial_sum = key_partial_sum + jnp.dot(grad_scores.T, query_rows, preferred_element_type=jnp.float32) * score_scale
        value_partial_sum = value_partial_sum + jnp.dot(probs.astype(jnp.bfloat16).T, grad_rows, preferred_element_type=jnp.float32)
        return ((key_partial_sum, value_partial_sum), (attended, grad_query))
    zeros = jnp.zeros((TOKEN_COUNT, HEAD_WIDTH), jnp.float32)
    (key_partial_sum, value_partial_sum), (attended, grad_query) = lax.scan(one_block, (zeros, zeros), jnp.arange(TOKEN_COUNT // size, dtype=jnp.int32))
    return (attended.reshape(TOKEN_COUNT, HEAD_WIDTH), grad_query.reshape(TOKEN_COUNT, HEAD_WIDTH), key_partial_sum, value_partial_sum)

def reference(queries, keys, values, grad_out, block_order):
    positions = stored_positions(block_order)
    query_group = QUERY_HEAD_COUNT // KEY_VALUE_HEADS
    query_heads = queries.reshape(TOKEN_COUNT, QUERY_HEAD_COUNT, HEAD_WIDTH).transpose(1, 0, 2)
    grad_heads = grad_out.reshape(TOKEN_COUNT, QUERY_HEAD_COUNT, HEAD_WIDTH).transpose(1, 0, 2)
    key_head_rows = keys.reshape(TOKEN_COUNT, KEY_VALUE_HEADS, HEAD_WIDTH).transpose(1, 0, 2)
    value_head_rows = values.reshape(TOKEN_COUNT, KEY_VALUE_HEADS, HEAD_WIDTH).transpose(1, 0, 2)

    def per_head(head):
        shared = head // query_group
        return head_pass(query_heads[head], key_head_rows[shared], value_head_rows[shared], grad_heads[head], positions)
    attended, grad_query, key_partial_sum, value_partial_sum = lax.map(per_head, jnp.arange(QUERY_HEAD_COUNT, dtype=jnp.int32))
    attended = attended.transpose(1, 0, 2).reshape(TOKEN_COUNT, QUERY_HEAD_COUNT * HEAD_WIDTH)
    grad_query = grad_query.transpose(1, 0, 2).reshape(TOKEN_COUNT, QUERY_HEAD_COUNT * HEAD_WIDTH)
    key_grand_total = key_partial_sum.reshape(KEY_VALUE_HEADS, query_group, TOKEN_COUNT, HEAD_WIDTH).sum(axis=1)
    value_grand_total = value_partial_sum.reshape(KEY_VALUE_HEADS, query_group, TOKEN_COUNT, HEAD_WIDTH).sum(axis=1)
    key_gradient = key_grand_total.transpose(1, 0, 2).reshape(TOKEN_COUNT, KEY_VALUE_HEADS * HEAD_WIDTH).astype(jnp.bfloat16)
    value_gradient = value_grand_total.transpose(1, 0, 2).reshape(TOKEN_COUNT, KEY_VALUE_HEADS * HEAD_WIDTH).astype(jnp.bfloat16)
    return (attended, grad_query, key_gradient, value_gradient)
```

```python
import functools
import math

import jax
import jax.numpy as jnp
from jax import lax
from jax.experimental import pallas as pl
from jax.experimental.pallas import tpu as pltpu
from jax.sharding import Mesh, PartitionSpec as P

D = 128
BLK = 32
G = 4
HEADS = 4
TB = 4
ROWS = TB * BLK * G
KB = 16
TK = KB * BLK
SCALE = 1.0 / math.sqrt(D)
C2 = SCALE * math.log2(math.e)
LOW = -1e30
F32, BF = jnp.float32, jnp.bfloat16
VMEM = pl.BlockSpec(memory_space=pltpu.VMEM)
SMEM = pl.BlockSpec(memory_space=pltpu.SMEM)


def mo(value, by):
    return pl.multiple_of(value, by)


def call(body, out_shape, n_smem, n_in, scratch=(), cost=None):
    return pl.pallas_call(
        body,
        out_shape=out_shape,
        in_specs=[SMEM] * n_smem + [VMEM] * n_in,
        out_specs=jax.tree.map(lambda _: VMEM, out_shape),
        scratch_shapes=list(scratch),
        compiler_params=pltpu.CompilerParams(vmem_limit_bytes=48 * 1024 * 1024),
        cost_estimate=cost,
    )


def sds(shape, dtype):
    return jax.ShapeDtypeStruct(shape, dtype)


def pack_body(head, q, k, v, g, *outs):
    sends, kv_out = outs[:HEADS], outs[HEADS]
    h = head[0]
    for x in range(HEADS):
        cols = pl.ds(mo((h ^ x) * (G * D), G * D), G * D)
        sends[x][:, : G * D] = q[:, cols]
        sends[x][:, G * D :] = g[:, cols]
    fan = kv_out.shape[0] // HEADS
    for j in range(HEADS):
        both = jnp.concatenate([k[:, j * D : (j + 1) * D], v[:, j * D : (j + 1) * D]], axis=1)
        for f in range(fan):
            kv_out[j * fan + f] = both


def tile_bounds(meta, nq, nk, t):
    q_at, k_at = nq + nk, 2 * nq + nk
    first, last = meta[q_at + t * TB], meta[q_at + t * TB + TB - 1]
    full, need = jnp.int32(0), jnp.int32(0)
    for j in range(nk // KB):
        need += (meta[k_at + j * KB] <= last).astype(jnp.int32)
        full += (meta[k_at + j * KB + KB - 1] < first).astype(jnp.int32)
    return full, need


def query_lane(meta, nq, nk, t):
    lane = lax.broadcasted_iota(jnp.int32, (1, ROWS), 1)
    block = (lane // BLK) % TB
    pos = jnp.zeros((1, ROWS), jnp.int32)
    for b in range(TB):
        pos = jnp.where(block == b, meta[nq + nk + t * TB + b], pos)
    return pos * BLK + lane % BLK


def masked_scores(meta, nq, nk, scores, lane_pos, j):
    row = lax.broadcasted_iota(jnp.int32, (BLK, ROWS), 0)
    parts = []
    for b in range(KB):
        at = meta[2 * nq + nk + j * KB + b] * BLK
        allowed = row <= lane_pos - at
        parts.append(jnp.where(allowed, scores[b * BLK : (b + 1) * BLK], LOW))
    return jnp.concatenate(parts, axis=0)


def dot(a, b):
    return lax.dot_general(a, b, (((1,), (0,)), ((), ())), preferred_element_type=F32)


def forward_body(cn, nk, meta, *refs):
    q_refs, kv = refs[:cn], refs[cn]
    stats, ot, qn, gn, qt, gt, ks, vs, kt = refs[cn + 1 : cn + 10]
    vt = refs[cn + 10]
    nq = cn * HEADS
    nt, nj = nq // TB, nk // KB
    for r in range(cn):
        for x in range(HEADS):
            n = meta[r * HEADS + x]
            base = (n // TB) * ROWS + (n % TB) * BLK
            for g in range(G):
                at = pl.ds(mo(base + g * TB * BLK, BLK), BLK)
                qn[at, :] = q_refs[r][x, :, g * D : (g + 1) * D]
                gn[at, :] = q_refs[r][x, :, (G + g) * D : (G + g + 1) * D]
    for s in range(nk):
        at = pl.ds(mo(meta[nq + s] * BLK, BLK), BLK)
        ks[at, :] = kv[s, :, :D]
        vs[at, :] = kv[s, :, D:]
    for t in range(nt):
        qt[t] = qn[t * ROWS : (t + 1) * ROWS, :].T
        gt[t] = gn[t * ROWS : (t + 1) * ROWS, :].T
    for j in range(nj):
        kt[j] = ks[j * TK : (j + 1) * TK, :].T
        vt[j] = vs[j * TK : (j + 1) * TK, :].T

    def tile(t, unused):
        full, need = tile_bounds(meta, nq, nk, t)
        lane_pos = query_lane(meta, nq, nk, t)
        query = qt[t]

        def step(masked, j, state):
            run, total, acc = state
            scores = dot(ks[pl.ds(mo(j * TK, TK), TK), :], query)
            if masked:
                scores = masked_scores(meta, nq, nk, scores, lane_pos, j)
            new = jnp.maximum(run, jnp.max(scores, axis=0, keepdims=True))
            weights = jnp.exp2(scores * C2 - new * C2)
            factor = jnp.exp2((run - new) * C2)
            total = total * factor + jnp.sum(weights, axis=0, keepdims=True)
            acc = acc * factor + dot(vt[j], weights.astype(BF))
            return new, total, acc

        state = (
            jnp.full((1, ROWS), LOW * 0.1, F32),
            jnp.zeros((1, ROWS), F32),
            jnp.zeros((D, ROWS), F32),
        )
        state = lax.fori_loop(0, full, functools.partial(step, False), state)
        run, total, acc = lax.fori_loop(full, need, functools.partial(step, True), state)
        some = total > 0.0
        safe = jnp.where(some, total, 1.0)
        inverse = jnp.where(some, 1.0 / safe, 0.0)
        out = acc * inverse
        lanes = pl.ds(mo(t * ROWS, ROWS), ROWS)
        stats[0:1, lanes] = jnp.where(some, run * C2 + jnp.log2(safe), LOW)
        stats[1:2, lanes] = jnp.sum(out * gt[t].astype(F32), axis=0, keepdims=True)
        ot[t] = out
        return unused

    lax.fori_loop(0, nt, tile, 0)


def backward_body(cn, nk, meta, *refs):
    stats = refs[:cn]
    ot, qn, gn, qt, gt, ks, vs, kt = refs[cn : cn + 8]
    kv_out, outs = refs[cn + 8], refs[cn + 9 : 2 * cn + 9]
    dk, dv, dqt, on, dqn, log_all, delta_all, own_part = refs[2 * cn + 9 :]
    nq = cn * HEADS
    nt = nq // TB

    logs = [s[0:1, :] for s in stats]
    top = functools.reduce(jnp.maximum, logs)
    parts = [jnp.exp2(l - top) for l in logs]
    whole = functools.reduce(jnp.add, parts)
    inverse = 1.0 / whole
    log_all[...] = top + jnp.log2(whole)
    delta_all[...] = functools.reduce(jnp.add, [p * s[1:2, :] for p, s in zip(parts, stats)]) * inverse
    own_part[...] = parts[0] * inverse
    dk[...] = jnp.zeros_like(dk)
    dv[...] = jnp.zeros_like(dv)

    def tile(t, unused):
        full, need = tile_bounds(meta, nq, nk, t)
        lane_pos = query_lane(meta, nq, nk, t)
        lanes = pl.ds(mo(t * ROWS, ROWS), ROWS)
        log_total, delta = log_all[:, lanes], delta_all[:, lanes]
        dqt[...] = jnp.zeros_like(dqt)

        def step(masked, j, state):
            keys = pl.ds(mo(j * TK, TK), TK)
            scores = dot(ks[keys, :], qt[t])
            if masked:
                scores = masked_scores(meta, nq, nk, scores, lane_pos, j)
            probs = jnp.exp2(scores * C2 - log_total)
            grad_probs = dot(vs[keys, :], gt[t])
            grad_scores = (probs * (grad_probs - delta)).astype(BF)
            dv[keys, :] += dot(probs.astype(BF), gn[lanes, :])
            dk[keys, :] += dot(grad_scores, qn[lanes, :])
            dqt[...] += dot(kt[j], grad_scores)
            return state

        lax.fori_loop(0, full, functools.partial(step, False), 0)
        lax.fori_loop(full, need, functools.partial(step, True), 0)
        dqn[lanes, :] = (dqt[...] * SCALE).T.astype(BF)
        on[lanes, :] = (ot[t] * own_part[:, lanes]).T.astype(BF)
        return unused

    lax.fori_loop(0, nt, tile, 0)
    for s in range(nk):
        at = pl.ds(mo(meta[nq + s] * BLK, BLK), BLK)
        kv_out[s, :, :D] = (dk[at, :] * SCALE).astype(BF)
        kv_out[s, :, D:] = dv[at, :].astype(BF)
    for r in range(cn):
        for x in range(HEADS):
            n = meta[r * HEADS + x]
            base = (n // TB) * ROWS + (n % TB) * BLK
            for g in range(G):
                at = pl.ds(mo(base + g * TB * BLK, BLK), BLK)
                outs[r][x, :, g * D : (g + 1) * D] = on[at, :]
                outs[r][x, :, (G + g) * D : (G + g + 1) * D] = dqn[at, :]


def sum_body(cn, *refs):
    parts, outs = refs[:cn], refs[cn:]
    for x in range(HEADS):
        total = parts[0][x].astype(F32)
        for part in parts[1:]:
            total += part[x].astype(F32)
        outs[x][...] = total.astype(BF)


def place_body(head, *refs):
    parts, attended, grad = refs[:HEADS], refs[HEADS], refs[HEADS + 1]
    h = head[0]
    for x in range(HEADS):
        cols = pl.ds(mo((h ^ x) * (G * D), G * D), G * D)
        attended[:, cols] = parts[x][:, : G * D]
        grad[:, cols] = parts[x][:, G * D :]


def key_sum_body(parts, dk, dv):
    fan = parts.shape[0] // HEADS
    for j in range(HEADS):
        total = parts[j * fan].astype(F32)
        for f in range(1, fan):
            total += parts[j * fan + f].astype(F32)
        dk[:, j * D : (j + 1) * D] = total[:, :D].astype(BF)
        dv[:, j * D : (j + 1) * D] = total[:, D:].astype(BF)


def flip(axis, value, x):
    return lax.ppermute(value, axis, [(j, j ^ x) for j in range(HEADS)])


SHARE_X = False


def per_device(queries, keys, values, grad_out, block_order):
    xs, zs, ys = lax.axis_size("xlo"), lax.axis_size("z"), lax.axis_size("inner")
    head, xlo = lax.axis_index("head"), lax.axis_index("xlo")
    z, inner = lax.axis_index("z"), lax.axis_index("inner")
    shifts = [(a, b) for a in range(xs if SHARE_X else 1) for b in range(ys)]
    key_axes = ("head", "z") if SHARE_X else ("head", "xlo", "z")
    cn = len(shifts)
    nq = cn * HEADS
    nk = HEADS * zs * (1 if SHARE_X else xs)

    def share(value, shift, back=False):
        a, b = shift
        pairs = []
        for i in range(xs):
            for j in range(ys):
                source, target = i * ys + j, ((i + a) % xs) * ys + (j + b) % ys
                pairs.append((target, source) if back else (source, target))
        return lax.ppermute(value, ("xlo", "inner"), pairs)

    def block_of(h, i, j, k):
        return ((h * xs + i) * zs + j) * ys + k

    slot = jnp.arange(nq, dtype=jnp.int32)
    shift_x = (slot // HEADS) // ys
    shift_y = (slot // HEADS) % ys
    q_block = block_of(head ^ (slot % HEADS), (xlo - shift_x) % xs, z, (inner - shift_y) % ys)
    slot = jnp.arange(nk, dtype=jnp.int32)
    k_x = xlo if SHARE_X else (slot // zs) % xs
    k_block = block_of(slot * HEADS // nk, k_x, slot % zs, inner)
    every = jnp.arange(block_order.shape[0], dtype=jnp.int32)

    def ranked(block):
        pos = jnp.sum(jnp.where(block[:, None] == every[None, :], block_order[None, :], 0), axis=1)
        rank = jnp.sum((pos[None, :] < pos[:, None]).astype(jnp.int32), axis=1)
        n = block.shape[0]
        hit = rank[None, :] == jnp.arange(n, dtype=jnp.int32)[:, None]
        return rank, jnp.sum(jnp.where(hit, pos[None, :], 0), axis=1)

    q_rank, q_sorted = ranked(q_block)
    k_rank, k_sorted = ranked(k_block)
    meta = jnp.concatenate([q_rank, k_rank, q_sorted, k_sorted])
    head_word = head[None].astype(jnp.int32)

    wide = sds((BLK, 2 * G * D), BF)
    packed = call(pack_body, (wide,) * HEADS + (sds((nk, BLK, 2 * D), BF),), 1, 4)(
        head_word, queries, keys, values, grad_out
    )
    with jax.named_scope("keys_in"):
        kv = lax.all_to_all(packed[HEADS], key_axes, split_axis=0, concat_axis=0, tiled=True)
    with jax.named_scope("queries_in"):
        mine = jnp.stack([packed[0]] + [flip("head", packed[x], x) for x in range(1, HEADS)])
        q_all = [mine] + [share(mine, shift) for shift in shifts[1:]]

    nrow, nkey = nq * BLK * G, nk * BLK
    nt, nj = nq // TB, nk // KB
    tiles = sds((nt, D, ROWS), BF)
    rows = sds((nrow, D), BF)
    key_rows = sds((nkey, D), BF)
    pairs = nrow * nkey
    stats, ot, *staged = call(
        functools.partial(forward_body, cn, nk),
        (sds((2, nrow), F32), sds((nt, D, ROWS), F32), rows, rows, tiles, tiles, key_rows, key_rows, sds((nj, D, TK), BF)),
        1,
        cn + 1,
        [pltpu.VMEM((nj, D, TK), BF)],
        pl.CostEstimate(flops=4 * pairs * D, bytes_accessed=1 << 22, transcendentals=pairs),
    )(meta, *q_all, kv)
    with jax.named_scope("stats"):
        all_stats = [stats] + [share(stats, shift) for shift in shifts[1:]]
    kv_part, *q_parts = call(
        functools.partial(backward_body, cn, nk),
        (sds((nk, BLK, 2 * D), BF),) + (sds((HEADS, BLK, 2 * G * D), BF),) * cn,
        1,
        cn + 8,
        [
            pltpu.VMEM((nkey, D), F32),
            pltpu.VMEM((nkey, D), F32),
            pltpu.VMEM((D, ROWS), F32),
            pltpu.VMEM((nrow, D), BF),
            pltpu.VMEM((nrow, D), BF),
            pltpu.VMEM((1, nrow), F32),
            pltpu.VMEM((1, nrow), F32),
            pltpu.VMEM((1, nrow), F32),
        ],
        pl.CostEstimate(flops=10 * pairs * D, bytes_accessed=1 << 22, transcendentals=pairs),
    )(meta, *all_stats, ot, *staged)
    with jax.named_scope("keys_out"):
        kv_parts = lax.all_to_all(kv_part, key_axes, split_axis=0, concat_axis=0, tiled=True)
    with jax.named_scope("queries_out"):
        back = [q_parts[0]] + [share(part, shift, True) for part, shift in zip(q_parts[1:], shifts[1:])]
        sums = call(functools.partial(sum_body, cn), (wide,) * HEADS, 0, cn)(*back)
        final = [sums[0]] + [flip("head", sums[x], x) for x in range(1, HEADS)]
        full = sds(queries.shape, BF)
        attended, grad_queries = call(place_body, (full, full), 1, HEADS)(head_word, *final)
    with jax.named_scope("key_sums"):
        thin = sds(keys.shape, BF)
        grad_keys, grad_values = call(key_sum_body, (thin, thin), 0, 1)(kv_parts)
    return attended, grad_queries, grad_keys, grad_values


def solution(mesh):
    heads, outer, inner = (mesh.shape[name] for name in ("head", "outer", "inner"))
    split = Mesh(mesh.devices.reshape(heads, 2, outer // 2, inner), ("head", "xlo", "z", "inner"))
    rows = P(("head", "xlo", "z", "inner"), None)
    return jax.shard_map(
        per_device,
        mesh=split,
        in_specs=(rows, rows, rows, rows, P()),
        out_specs=(rows, rows, rows, rows),
        check_vma=False,
    )
```

```python
import functools
import math

import jax
import jax.numpy as jnp
from jax import lax
from jax.experimental import pallas as pl
from jax.experimental.pallas import tpu as pltpu
from jax.sharding import Mesh, PartitionSpec as P

D = 128
BLK = 32
G = 4
HEADS = 4
TB = 4
ROWS = TB * BLK * G
KB = 16
TK = KB * BLK
KBF = 32
TKF = KBF * BLK
SUB = 256
SCALE = 1.0 / math.sqrt(D)
C2 = SCALE * math.log2(math.e)
LOW = -1e30
LIMIT = 20 * 1024 * 1024
F32, BF = jnp.float32, jnp.bfloat16
VMEM = pl.BlockSpec(memory_space=pltpu.VMEM)
HBM = pl.BlockSpec(memory_space=pltpu.HBM)
SMEM = pl.BlockSpec(memory_space=pltpu.SMEM)


def mo(value, by):
    return pl.multiple_of(value, by)


def call(body, out_shape, n_smem, n_in, scratch=(), cost=None, space=VMEM, limit=LIMIT):
    return pl.pallas_call(
        body,
        out_shape=out_shape,
        in_specs=[SMEM] * n_smem + [space] * n_in,
        out_specs=jax.tree.map(lambda _: VMEM, out_shape),
        scratch_shapes=list(scratch),
        compiler_params=pltpu.CompilerParams(vmem_limit_bytes=limit),
        cost_estimate=cost,
    )


def sds(shape, dtype):
    return jax.ShapeDtypeStruct(shape, dtype)


def pack_body(head, q_in, k_in, v_in, g_in, *refs):
    q_out, g_out, kv_out = refs[:HEADS], refs[HEADS : 2 * HEADS], refs[2 * HEADS]
    q, k, v, g, sems = refs[2 * HEADS + 1 :]
    copies = [
        pltpu.make_async_copy(source, target, sems.at[n])
        for n, (source, target) in enumerate(((k_in, k), (v_in, v), (q_in, q), (g_in, g)))
    ]
    for copy in copies:
        copy.start()
    copies[0].wait()
    copies[1].wait()
    fan = kv_out.shape[0] // HEADS
    for j in range(HEADS):
        both = jnp.concatenate([k[:, j * D : (j + 1) * D], v[:, j * D : (j + 1) * D]], axis=1)
        for f in range(fan):
            kv_out[j * fan + f] = both
    h = head[0]
    for copy, rows, outs in ((copies[2], q, q_out), (copies[3], g, g_out)):
        copy.wait()
        for x in range(HEADS):
            outs[x][...] = rows[:, pl.ds(mo((h ^ x) * (G * D), G * D), G * D)]


def tile_bounds(meta, nq, nk, t, kb):
    q_at, k_at = nq + nk, 2 * nq + nk
    first, last = meta[q_at + t * TB], meta[q_at + t * TB + TB - 1]
    full, need = jnp.int32(0), jnp.int32(0)
    for j in range(nk // kb):
        need += (meta[k_at + j * kb] <= last).astype(jnp.int32)
        full += (meta[k_at + j * kb + kb - 1] < first).astype(jnp.int32)
    return full, need


def query_lane(meta, nq, nk, t):
    lane = lax.broadcasted_iota(jnp.int32, (1, ROWS), 1)
    block = (lane // BLK) % TB
    pos = jnp.zeros((1, ROWS), jnp.int32)
    for b in range(TB):
        pos = jnp.where(block == b, meta[nq + nk + t * TB + b], pos)
    return pos * BLK + lane % BLK


def masked_scores(meta, nq, nk, scores, lane_pos, first):
    row = lax.broadcasted_iota(jnp.int32, (BLK, ROWS), 0)
    parts = []
    for b in range(scores.shape[0] // BLK):
        at = meta[2 * nq + nk + first + b] * BLK
        allowed = row <= lane_pos - at
        parts.append(jnp.where(allowed, scores[b * BLK : (b + 1) * BLK], LOW))
    return jnp.concatenate(parts, axis=0)


def dot(a, b):
    return lax.dot_general(a, b, (((1,), (0,)), ((), ())), preferred_element_type=F32)


def row_slots(meta, cn):
    for r in range(cn):
        for x in range(HEADS):
            n = meta[r * HEADS + x]
            yield r, x, (n // TB) * ROWS + (n % TB) * BLK


def rows_at(base, g):
    return pl.ds(mo(base + g * TB * BLK, BLK), BLK)


def stage_body(cn, meta, *refs):
    parts, (rows, tiles) = refs[:cn], refs[cn:]
    for r, x, base in row_slots(meta, cn):
        for g in range(G):
            rows[rows_at(base, g), :] = parts[r][x, :, g * D : (g + 1) * D]
    for t in range(tiles.shape[0]):
        tiles[t] = rows[t * ROWS : (t + 1) * ROWS, :].T


def forward_scratch(nk):
    return [pltpu.VMEM((nk // KBF, D, TKF), BF), pltpu.VMEM((nk * BLK, ROWS), F32)]


def forward_body(cn, nk, meta, qt, kv, logs, ot, ks, vs, weights_out, vt, sbuf):
    nq = cn * HEADS
    nt, nj = nq // TB, nk // KBF
    for s in range(nk):
        at = pl.ds(mo(meta[nq + s] * BLK, BLK), BLK)
        ks[at, :] = kv[s, :, :D]
        vs[at, :] = kv[s, :, D:]
    for j in range(nj):
        vt[j] = vs[j * TKF : (j + 1) * TKF, :].T

    def tile(t, unused):
        full, need = tile_bounds(meta, nq, nk, t, KBF)
        lane_pos = query_lane(meta, nq, nk, t)
        query = qt[t]

        def score(masked, j, run):
            for c in range(TKF // SUB):
                at = pl.ds(mo(j * TKF + c * SUB, SUB), SUB)
                scores = dot(ks[at, :], query)
                if masked:
                    scores = masked_scores(meta, nq, nk, scores, lane_pos, j * KBF + c * (SUB // BLK))
                sbuf[at, :] = scores
                run = jnp.maximum(run, jnp.max(scores, axis=0, keepdims=True))
            return run

        run = jnp.full((1, ROWS), LOW * 0.1, F32)
        run = lax.fori_loop(0, full, functools.partial(score, False), run)
        run = lax.fori_loop(full, need, functools.partial(score, True), run)
        top = run * C2

        def step(j, state):
            total, acc = state
            for c in range(TKF // SUB):
                at = pl.ds(mo(j * TKF + c * SUB, SUB), SUB)
                weights = jnp.exp2(sbuf[at, :] * C2 - top)
                total += jnp.sum(weights, axis=0, keepdims=True)
                rounded = weights.astype(BF)
                weights_out[t, at, :] = rounded
                acc += dot(vt[j, :, c * SUB : (c + 1) * SUB], rounded)
            return total, acc

        state = (jnp.zeros((1, ROWS), F32), jnp.zeros((D, ROWS), F32))
        total, acc = lax.fori_loop(0, need, step, state)
        some = total > 0.0
        safe = jnp.where(some, total, 1.0)
        lanes = pl.ds(mo(t * ROWS, ROWS), ROWS)
        logs[0:1, lanes] = jnp.where(some, top + jnp.log2(safe), LOW)
        logs[1:2, lanes] = top
        ot[t] = acc * jnp.where(some, 1.0 / safe, 0.0)
        return unused

    lax.fori_loop(0, nt, tile, 0)


def delta_body(cn, meta, logs, ot, *refs):
    parts, (stats, gt, gn) = refs[:cn], refs[cn:]
    for r, x, base in row_slots(meta, cn):
        for g in range(G):
            gn[rows_at(base, g), :] = parts[r][x, :, g * D : (g + 1) * D]
    stats[0:1, :] = logs[0:1, :]
    for t in range(gt.shape[0]):
        lanes = slice(t * ROWS, (t + 1) * ROWS)
        grads = gn[lanes, :].T
        gt[t] = grads
        stats[1:2, lanes] = jnp.sum(ot[t] * grads.astype(F32), axis=0, keepdims=True)


def attended_body(cn, meta, ot, *refs):
    outs, on = refs[:cn], refs[cn]
    for t in range(ot.shape[0]):
        on[t * ROWS : (t + 1) * ROWS, :] = ot[t].T.astype(BF)
    for r, x, base in row_slots(meta, cn):
        for g in range(G):
            outs[r][x, :, g * D : (g + 1) * D] = on[rows_at(base, g), :]


def combine(stats):
    logs = [s[0:1, :] for s in stats]
    top = functools.reduce(jnp.maximum, logs)
    parts = [jnp.exp2(log - top) for log in logs]
    whole = functools.reduce(jnp.add, parts)
    return parts, whole, top


def backward_body(cn, nk, meta, *refs):
    stats = refs[:cn]
    logs, qn, gt, ks, vs, weights = refs[cn : cn + 6]
    kv_out, outs = refs[cn + 6], refs[cn + 7 : 2 * cn + 7]
    dk, dv, dqt, dqn, gn, scale_all, delta_all, kt = refs[2 * cn + 7 :]
    nq = cn * HEADS
    nt = nq // TB

    for j in range(nk // KB):
        kt[j] = ks[j * TK : (j + 1) * TK, :].T
    parts, whole, top = combine(stats)
    scale_all[...] = jnp.exp2(logs[1:2, :] - top) / whole
    delta_all[...] = functools.reduce(jnp.add, [p * s[1:2, :] for p, s in zip(parts, stats)]) / whole
    dk[...] = jnp.zeros_like(dk)
    dv[...] = jnp.zeros_like(dv)

    def tile(t, unused):
        full, need = tile_bounds(meta, nq, nk, t, KB)
        lanes = pl.ds(mo(t * ROWS, ROWS), ROWS)
        scale, delta = scale_all[:, lanes], delta_all[:, lanes]
        gn[...] = (gt[t].astype(F32) * scale).T.astype(BF)
        dqt[...] = jnp.zeros_like(dqt)

        def step(j, state):
            for c in range(TK // SUB):
                keys = pl.ds(mo(j * TK + c * SUB, SUB), SUB)
                own = weights[t, keys, :]
                lean = (dot(vs[keys, :], gt[t]) - delta) * scale
                grad_scores = (own.astype(F32) * lean).astype(BF)
                dv[keys, :] += dot(own, gn[...])
                dk[keys, :] += dot(grad_scores, qn[lanes, :])
                dqt[...] += dot(kt[j, :, c * SUB : (c + 1) * SUB], grad_scores)
            return state

        lax.fori_loop(0, need, step, 0)
        dqn[lanes, :] = (dqt[...] * SCALE).T.astype(BF)
        return unused

    lax.fori_loop(0, nt, tile, 0)
    for s in range(nk):
        at = pl.ds(mo(meta[nq + s] * BLK, BLK), BLK)
        kv_out[s, :, :D] = (dk[at, :] * SCALE).astype(BF)
        kv_out[s, :, D:] = dv[at, :].astype(BF)
    for r, x, base in row_slots(meta, cn):
        for g in range(G):
            outs[r][x, :, g * D : (g + 1) * D] = dqn[rows_at(base, g), :]


def sum_body(cn, meta, *refs):
    stats, attended, grads = refs[:cn], refs[cn : 2 * cn], refs[2 * cn : 3 * cn]
    outs, columns = refs[3 * cn : 3 * cn + HEADS], refs[3 * cn + HEADS]
    parts, whole, top = combine(stats)
    inverse = 1.0 / whole
    spread = D // cn
    tall = jnp.concatenate([jnp.broadcast_to(p * inverse, (spread, p.shape[1])) for p in parts], axis=0)
    for t in range(tall.shape[1] // ROWS):
        columns[t * ROWS : (t + 1) * ROWS, :] = tall[:, t * ROWS : (t + 1) * ROWS].T
    for r, x, base in row_slots(meta, 1):
        for g in range(G):
            cols = slice(g * D, (g + 1) * D)
            column = columns[rows_at(base, g), :]
            total = jnp.zeros((BLK, D), F32)
            for i in range(cn):
                total += column[:, i * spread : i * spread + 1] * attended[i][x, :, cols].astype(F32)
            outs[x][:, cols] = total.astype(BF)
        total = grads[0][x].astype(F32)
        for i in range(1, cn):
            total += grads[i][x].astype(F32)
        outs[x][:, G * D :] = total.astype(BF)


def place_body(head, *refs):
    parts, attended, grad = refs[:HEADS], refs[HEADS], refs[HEADS + 1]
    h = head[0]
    for x in range(HEADS):
        cols = pl.ds(mo((h ^ x) * (G * D), G * D), G * D)
        attended[:, cols] = parts[x][:, : G * D]
        grad[:, cols] = parts[x][:, G * D :]


def key_sum_body(parts, dk, dv):
    fan = parts.shape[0] // HEADS
    for j in range(HEADS):
        total = parts[j * fan].astype(F32)
        for f in range(1, fan):
            total += parts[j * fan + f].astype(F32)
        dk[:, j * D : (j + 1) * D] = total[:, :D].astype(BF)
        dv[:, j * D : (j + 1) * D] = total[:, D:].astype(BF)


def flip(axis, value, x):
    return lax.ppermute(value, axis, [(j, j ^ x) for j in range(HEADS)])


SHARE_X = False


def per_device(queries, keys, values, grad_out, block_order):
    xs, zs, ys = lax.axis_size("xlo"), lax.axis_size("z"), lax.axis_size("inner")
    head, xlo = lax.axis_index("head"), lax.axis_index("xlo")
    z, inner = lax.axis_index("z"), lax.axis_index("inner")
    shifts = [(a, b) for a in range(xs if SHARE_X else 1) for b in range(ys)]
    key_axes = ("head", "z") if SHARE_X else ("head", "xlo", "z")
    cn = len(shifts)
    nq = cn * HEADS
    nk = HEADS * zs * (1 if SHARE_X else xs)

    def share(value, shift, back=False):
        a, b = shift
        pairs = []
        for i in range(xs):
            for j in range(ys):
                source, target = i * ys + j, ((i + a) % xs) * ys + (j + b) % ys
                pairs.append((target, source) if back else (source, target))
        return lax.ppermute(value, ("xlo", "inner"), pairs)

    def block_of(h, i, j, k):
        return ((h * xs + i) * zs + j) * ys + k

    slot = jnp.arange(nq, dtype=jnp.int32)
    shift_x = (slot // HEADS) // ys
    shift_y = (slot // HEADS) % ys
    q_block = block_of(head ^ (slot % HEADS), (xlo - shift_x) % xs, z, (inner - shift_y) % ys)
    slot = jnp.arange(nk, dtype=jnp.int32)
    k_x = xlo if SHARE_X else (slot // zs) % xs
    k_block = block_of(slot * HEADS // nk, k_x, slot % zs, inner)
    every = jnp.arange(block_order.shape[0], dtype=jnp.int32)

    def ranked(block):
        pos = jnp.sum(jnp.where(block[:, None] == every[None, :], block_order[None, :], 0), axis=1)
        rank = jnp.sum((pos[None, :] < pos[:, None]).astype(jnp.int32), axis=1)
        n = block.shape[0]
        hit = rank[None, :] == jnp.arange(n, dtype=jnp.int32)[:, None]
        return rank, jnp.sum(jnp.where(hit, pos[None, :], 0), axis=1)

    q_rank, q_sorted = ranked(q_block)
    k_rank, k_sorted = ranked(k_block)
    meta = jnp.concatenate([q_rank, k_rank, q_sorted, k_sorted])
    head_word = head[None].astype(jnp.int32)

    wide, half = sds((BLK, 2 * G * D), BF), sds((BLK, G * D), BF)
    full_in, thin_in = pltpu.VMEM(queries.shape, BF), pltpu.VMEM(keys.shape, BF)
    *packed, kv_send = call(
        pack_body,
        (half,) * (2 * HEADS) + (sds((nk, BLK, 2 * D), BF),),
        1,
        4,
        [full_in, thin_in, thin_in, full_in, pltpu.SemaphoreType.DMA((4,))],
        space=HBM,
        limit=60 * 1024 * 1024,
    )(head_word, queries, keys, values, grad_out)
    q_sends, g_sends = packed[:HEADS], packed[HEADS:]
    with jax.named_scope("keys_in"):
        kv = lax.all_to_all(kv_send, key_axes, split_axis=0, concat_axis=0, tiled=True)

    def gather(sends, after=None):
        mine = jnp.stack([sends[0]] + [flip("head", sends[x], x) for x in range(1, HEADS)])
        if after is not None:
            mine, _ = lax.optimization_barrier((mine, after))
        return [mine] + [share(mine, shift) for shift in shifts[1:]]

    nrow, nkey = nq * BLK * G, nk * BLK
    nt, nj = nq // TB, nk // KB
    tiles = sds((nt, D, ROWS), BF)
    rows = sds((nrow, D), BF)
    key_rows = sds((nkey, D), BF)
    pairs = sds((nt, nkey, ROWS), BF)
    stat = sds((2, nrow), F32)
    work = nrow * nkey
    with jax.named_scope("queries_in"):
        q_all = gather(q_sends)
        qn, qt = call(functools.partial(stage_body, cn), (rows, tiles), 1, cn)(meta, *q_all)
    with jax.named_scope("grads_in"):
        g_sends, _ = lax.optimization_barrier((tuple(g_sends), q_all[0]))
        g_all = gather(g_sends, qt)
    logs, ot, ks, vs, weights = call(
        functools.partial(forward_body, cn, nk),
        (stat, sds((nt, D, ROWS), F32), key_rows, key_rows, pairs),
        1,
        2,
        forward_scratch(nk),
        pl.CostEstimate(flops=4 * work * D, bytes_accessed=1 << 22, transcendentals=work),
    )(meta, qt, kv)
    stats, gt = call(
        functools.partial(delta_body, cn), (stat, tiles), 1, cn + 2, [pltpu.VMEM((nrow, D), BF)]
    )(meta, logs, ot, *g_all)
    with jax.named_scope("stats"):
        all_stats = [stats] + [share(stats, shift) for shift in shifts[1:]]
    with jax.named_scope("attended_out"):
        quad = sds((HEADS, BLK, G * D), BF)
        late_ot, _ = lax.optimization_barrier((ot, stats))
        o_parts = call(
            functools.partial(attended_body, cn), (quad,) * cn, 1, 1, [pltpu.VMEM((nrow, D), BF)],
            pl.CostEstimate(flops=0, bytes_accessed=1 << 22, transcendentals=0),
        )(meta, late_ot)
    with jax.named_scope("attended_out"):
        o_back = [o_parts[0]] + [share(part, shift, True) for part, shift in zip(o_parts[1:], shifts[1:])]
    kv_part, *q_parts = call(
        functools.partial(backward_body, cn, nk),
        (sds((nk, BLK, 2 * D), BF),) + (quad,) * cn,
        1,
        cn + 6,
        [
            pltpu.VMEM((nkey, D), F32),
            pltpu.VMEM((nkey, D), F32),
            pltpu.VMEM((D, ROWS), F32),
            pltpu.VMEM((nrow, D), BF),
            pltpu.VMEM((ROWS, D), BF),
            pltpu.VMEM((1, nrow), F32),
            pltpu.VMEM((1, nrow), F32),
            pltpu.VMEM((nj, D, TK), BF),
        ],
        pl.CostEstimate(flops=8 * work * D, bytes_accessed=1 << 22, transcendentals=0),
    )(meta, *all_stats, logs, qn, gt, ks, vs, weights)
    with jax.named_scope("keys_out"):
        kv_part, o_back = lax.optimization_barrier((kv_part, o_back))
        kv_parts = lax.all_to_all(kv_part, key_axes, split_axis=0, concat_axis=0, tiled=True)
    opposite = [shifts.index(((-a) % xs, (-b) % ys)) for a, b in shifts]
    with jax.named_scope("queries_out"):
        back = [q_parts[0]] + [share(part, shift, True) for part, shift in zip(q_parts[1:], shifts[1:])]
        sums = call(
            functools.partial(sum_body, cn), (wide,) * HEADS, 1, 3 * cn, [pltpu.VMEM((nrow, D), F32)]
        )(meta, *[all_stats[i] for i in opposite], *o_back, *back)
        final = [sums[0]] + [flip("head", sums[x], x) for x in range(1, HEADS)]
        full = sds(queries.shape, BF)
        attended, grad_queries = call(place_body, (full, full), 1, HEADS)(head_word, *final)
    with jax.named_scope("key_sums"):
        thin = sds(keys.shape, BF)
        grad_keys, grad_values = call(key_sum_body, (thin, thin), 0, 1)(kv_parts)
    return attended, grad_queries, grad_keys, grad_values


def solution(mesh):
    heads, outer, inner = (mesh.shape[name] for name in ("head", "outer", "inner"))
    split = Mesh(mesh.devices.reshape(heads, 2, outer // 2, inner), ("head", "xlo", "z", "inner"))
    rows = P(("head", "xlo", "z", "inner"), None)
    return jax.shard_map(
        per_device,
        mesh=split,
        in_specs=(rows, rows, rows, rows, P()),
        out_specs=(rows, rows, rows, rows),
        check_vma=False,
    )
```

```python
import functools
import math

import jax
import jax.numpy as jnp
from jax import lax
from jax.experimental import pallas as pl
from jax.experimental.pallas import tpu as pltpu
from jax.sharding import Mesh, PartitionSpec as P

D = 128
BLK = 32
G = 4
HEADS = 4
TB = 4
ROWS = TB * BLK * G
KB = 16
TK = KB * BLK
KBF = 32
TKF = KBF * BLK
SUB = 256
SCALE = 1.0 / math.sqrt(D)
C2 = SCALE * math.log2(math.e)
LOW = -1e30
XAXES = ("xhi", "xlo")
LIMIT = 20 * 1024 * 1024
F32, BF = jnp.float32, jnp.bfloat16
VMEM = pl.BlockSpec(memory_space=pltpu.VMEM)
HBM = pl.BlockSpec(memory_space=pltpu.HBM)
SMEM = pl.BlockSpec(memory_space=pltpu.SMEM)


def mo(value, by):
    return pl.multiple_of(value, by)


def call(body, out_shape, n_smem, n_in, scratch=(), cost=None, space=VMEM, limit=LIMIT):
    return pl.pallas_call(
        body,
        out_shape=out_shape,
        in_specs=[SMEM] * n_smem + [space] * n_in,
        out_specs=jax.tree.map(lambda _: VMEM, out_shape),
        scratch_shapes=list(scratch),
        compiler_params=pltpu.CompilerParams(vmem_limit_bytes=limit),
        cost_estimate=cost,
    )


def sds(shape, dtype):
    return jax.ShapeDtypeStruct(shape, dtype)


def pack_body(head, q_in, k_in, v_in, g_in, *refs):
    sends, kv_out = refs[:HEADS], refs[HEADS]
    q, k, v, g, sems = refs[HEADS + 1 :]
    copies = [
        pltpu.make_async_copy(source, target, sems.at[n])
        for n, (source, target) in enumerate(((k_in, k), (v_in, v), (q_in, q), (g_in, g)))
    ]
    for copy in copies:
        copy.start()
    copies[0].wait()
    copies[1].wait()
    fan = kv_out.shape[0] // HEADS
    for j in range(HEADS):
        both = jnp.concatenate([k[:, j * D : (j + 1) * D], v[:, j * D : (j + 1) * D]], axis=1)
        for f in range(fan):
            kv_out[j * fan + f] = both
    h = head[0]
    copies[2].wait()
    copies[3].wait()
    for x in range(HEADS):
        cols = pl.ds(mo((h ^ x) * (G * D), G * D), G * D)
        sends[x][:, : G * D] = q[:, cols]
        sends[x][:, G * D :] = g[:, cols]


def collect_body(*refs):
    parts, (queries, grads) = refs[:HEADS], refs[HEADS:]
    for x in range(HEADS):
        queries[x] = parts[x][:, : G * D]
        grads[x] = parts[x][:, G * D :]


def tile_bounds(meta, nq, nk, t, kb):
    q_at, k_at = nq + nk, 2 * nq + nk
    first, last = meta[q_at + t * TB], meta[q_at + t * TB + TB - 1]
    full, need = jnp.int32(0), jnp.int32(0)
    for j in range(nk // kb):
        need += (meta[k_at + j * kb] <= last).astype(jnp.int32)
        full += (meta[k_at + j * kb + kb - 1] < first).astype(jnp.int32)
    return full, need


def query_lane(meta, nq, nk, t):
    lane = lax.broadcasted_iota(jnp.int32, (1, ROWS), 1)
    block = (lane // BLK) % TB
    pos = jnp.zeros((1, ROWS), jnp.int32)
    for b in range(TB):
        pos = jnp.where(block == b, meta[nq + nk + t * TB + b], pos)
    return pos * BLK + lane % BLK


def masked_scores(meta, nq, nk, scores, lane_pos, first):
    row = lax.broadcasted_iota(jnp.int32, (BLK, ROWS), 0)
    parts = []
    for b in range(scores.shape[0] // BLK):
        at = meta[2 * nq + nk + first + b] * BLK
        allowed = row <= lane_pos - at
        parts.append(jnp.where(allowed, scores[b * BLK : (b + 1) * BLK], LOW))
    return jnp.concatenate(parts, axis=0)


def dot(a, b):
    return lax.dot_general(a, b, (((1,), (0,)), ((), ())), preferred_element_type=F32)


def row_slots(meta, cn):
    for r in range(cn):
        for x in range(HEADS):
            n = meta[r * HEADS + x]
            yield r, x, (n // TB) * ROWS + (n % TB) * BLK


def rows_at(base, g):
    return pl.ds(mo(base + g * TB * BLK, BLK), BLK)


def stage_body(cn, meta, *refs):
    parts, (rows, tiles) = refs[:cn], refs[cn:]
    for r, x, base in row_slots(meta, cn):
        for g in range(G):
            rows[rows_at(base, g), :] = parts[r][x, :, g * D : (g + 1) * D]
    for t in range(tiles.shape[0]):
        tiles[t] = rows[t * ROWS : (t + 1) * ROWS, :].T


def forward_scratch(nk):
    return [pltpu.VMEM((nk // KBF, D, TKF), BF), pltpu.VMEM((nk * BLK, ROWS), F32)]


def forward_body(cn, nk, meta, qt, kv_near, kv_far, logs, ot, ks, vs, weights_out, vt, sbuf):
    nq = cn * HEADS
    nt, nj = nq // TB, nk // KBF
    for s in range(nk):
        at = pl.ds(mo(meta[nq + s] * BLK, BLK), BLK)
        kv = (kv_near, kv_far)[s // (nk // 2)]
        ks[at, :] = kv[s % (nk // 2), :, :D]
        vs[at, :] = kv[s % (nk // 2), :, D:]
    for j in range(nj):
        vt[j] = vs[j * TKF : (j + 1) * TKF, :].T

    def tile(t, unused):
        full, need = tile_bounds(meta, nq, nk, t, KBF)
        lane_pos = query_lane(meta, nq, nk, t)
        query = qt[t]

        def score(masked, j, run):
            for c in range(TKF // SUB):
                at = pl.ds(mo(j * TKF + c * SUB, SUB), SUB)
                scores = dot(ks[at, :], query)
                if masked:
                    scores = masked_scores(meta, nq, nk, scores, lane_pos, j * KBF + c * (SUB // BLK))
                sbuf[at, :] = scores
                run = jnp.maximum(run, jnp.max(scores, axis=0, keepdims=True))
            return run

        run = jnp.full((1, ROWS), LOW * 0.1, F32)
        run = lax.fori_loop(0, full, functools.partial(score, False), run)
        run = lax.fori_loop(full, need, functools.partial(score, True), run)
        top = run * C2

        def step(j, state):
            total, acc = state
            for c in range(TKF // SUB):
                at = pl.ds(mo(j * TKF + c * SUB, SUB), SUB)
                weights = jnp.exp2(sbuf[at, :] * C2 - top)
                total += jnp.sum(weights, axis=0, keepdims=True)
                rounded = weights.astype(BF)
                weights_out[t, at, :] = rounded
                acc += dot(vt[j, :, c * SUB : (c + 1) * SUB], rounded)
            return total, acc

        state = (jnp.zeros((1, ROWS), F32), jnp.zeros((D, ROWS), F32))
        total, acc = lax.fori_loop(0, need, step, state)
        some = total > 0.0
        safe = jnp.where(some, total, 1.0)
        lanes = pl.ds(mo(t * ROWS, ROWS), ROWS)
        logs[0:1, lanes] = jnp.where(some, top + jnp.log2(safe), LOW)
        logs[1:2, lanes] = top
        ot[t] = acc * jnp.where(some, 1.0 / safe, 0.0)
        return unused

    lax.fori_loop(0, nt, tile, 0)


def delta_body(cn, meta, logs, ot, *refs):
    parts, (stats, gt, gn) = refs[:cn], refs[cn:]
    for r, x, base in row_slots(meta, cn):
        for g in range(G):
            gn[rows_at(base, g), :] = parts[r][x, :, g * D : (g + 1) * D]
    stats[0:1, :] = logs[0:1, :]
    for t in range(gt.shape[0]):
        lanes = slice(t * ROWS, (t + 1) * ROWS)
        grads = gn[lanes, :].T
        gt[t] = grads
        stats[1:2, lanes] = jnp.sum(ot[t] * grads.astype(F32), axis=0, keepdims=True)


def attended_body(ot, on):
    for t in range(ot.shape[0]):
        on[t * ROWS : (t + 1) * ROWS, :] = ot[t].T.astype(BF)


def combine(stats):
    logs = [s[0:1, :] for s in stats]
    top = functools.reduce(jnp.maximum, logs)
    parts = [jnp.exp2(log - top) for log in logs]
    whole = functools.reduce(jnp.add, parts)
    return parts, whole, top


def backward_body(cn, nk, meta, *refs):
    stats = refs[:cn]
    logs, qn, gt, ks, vs, weights, on = refs[cn : cn + 7]
    near, far, *outs = refs[cn + 7 : 2 * cn + 9]
    dk, dv, dqt, dqn, gn, scale_all, delta_all, kt = refs[2 * cn + 9 :]
    nq = cn * HEADS
    nt = nq // TB

    for j in range(nk // KB):
        kt[j] = ks[j * TK : (j + 1) * TK, :].T
    parts, whole, top = combine(stats)
    scale_all[...] = jnp.exp2(logs[1:2, :] - top) / whole
    delta_all[...] = functools.reduce(jnp.add, [p * s[1:2, :] for p, s in zip(parts, stats)]) / whole
    dk[...] = jnp.zeros_like(dk)
    dv[...] = jnp.zeros_like(dv)

    def tile(t, unused):
        full, need = tile_bounds(meta, nq, nk, t, KB)
        lanes = pl.ds(mo(t * ROWS, ROWS), ROWS)
        scale, delta = scale_all[:, lanes], delta_all[:, lanes]
        gn[...] = (gt[t].astype(F32) * scale).T.astype(BF)
        dqt[...] = jnp.zeros_like(dqt)

        def step(j, state):
            for c in range(TK // SUB):
                keys = pl.ds(mo(j * TK + c * SUB, SUB), SUB)
                own = weights[t, keys, :]
                lean = (dot(vs[keys, :], gt[t]) - delta) * scale
                grad_scores = (own.astype(F32) * lean).astype(BF)
                dv[keys, :] += dot(own, gn[...])
                dk[keys, :] += dot(grad_scores, qn[lanes, :])
                dqt[...] += dot(kt[j, :, c * SUB : (c + 1) * SUB], grad_scores)
            return state

        lax.fori_loop(0, need, step, 0)
        dqn[lanes, :] = (dqt[...] * SCALE).T.astype(BF)
        return unused

    lax.fori_loop(0, nt, tile, 0)
    for s in range(nk):
        at = pl.ds(mo(meta[nq + s] * BLK, BLK), BLK)
        kv_out = (near, far)[s // (nk // 2)]
        kv_out[s % (nk // 2), :, :D] = (dk[at, :] * SCALE).astype(BF)
        kv_out[s % (nk // 2), :, D:] = dv[at, :].astype(BF)
    for r, x, base in row_slots(meta, cn):
        for g in range(G):
            outs[r][x, :, g * D : (g + 1) * D] = on[rows_at(base, g), :]
            outs[r][x, :, (G + g) * D : (G + g + 1) * D] = dqn[rows_at(base, g), :]


def add_body(one, two, out):
    out[...] = (one[...].astype(F32) + two[...].astype(F32)).astype(BF)


def sum_body(cn, meta, *refs):
    stats, shares = refs[:cn], refs[cn : 2 * cn]
    outs, columns = refs[2 * cn : 2 * cn + HEADS], refs[2 * cn + HEADS]
    parts, whole, top = combine(stats)
    inverse = 1.0 / whole
    spread = D // cn
    tall = jnp.concatenate([jnp.broadcast_to(p * inverse, (spread, p.shape[1])) for p in parts], axis=0)
    for t in range(tall.shape[1] // ROWS):
        columns[t * ROWS : (t + 1) * ROWS, :] = tall[:, t * ROWS : (t + 1) * ROWS].T
    for r, x, base in row_slots(meta, 1):
        for g in range(G):
            cols = slice(g * D, (g + 1) * D)
            column = columns[rows_at(base, g), :]
            total = jnp.zeros((BLK, D), F32)
            for i in range(cn):
                total += column[:, i * spread : i * spread + 1] * shares[i][x, :, cols].astype(F32)
            outs[x][:, cols] = total.astype(BF)
        total = shares[0][x, :, G * D :].astype(F32)
        for i in range(1, cn):
            total += shares[i][x, :, G * D :].astype(F32)
        outs[x][:, G * D :] = total.astype(BF)


def place_body(head, *refs):
    parts, attended, grad = refs[:HEADS], refs[HEADS], refs[HEADS + 1]
    h = head[0]
    for x in range(HEADS):
        cols = pl.ds(mo((h ^ x) * (G * D), G * D), G * D)
        attended[:, cols] = parts[x][:, : G * D]
        grad[:, cols] = parts[x][:, G * D :]


def key_sum_body(parts, dk, dv):
    fan = parts.shape[0] // HEADS
    for j in range(HEADS):
        total = parts[j * fan].astype(F32)
        for f in range(1, fan):
            total += parts[j * fan + f].astype(F32)
        dk[:, j * D : (j + 1) * D] = total[:, :D].astype(BF)
        dv[:, j * D : (j + 1) * D] = total[:, D:].astype(BF)


def flip(axis, value, x):
    return lax.ppermute(value, axis, [(j, j ^ x) for j in range(HEADS)])


def per_device(queries, keys, values, grad_out, block_order):
    xs, zs, ys = lax.axis_size("xlo"), lax.axis_size("z"), lax.axis_size("inner")
    head, core = lax.axis_index(XAXES), lax.axis_index("core")
    z, inner = lax.axis_index("z"), lax.axis_index("inner")
    shifts = range(ys)
    cn = ys
    nq = cn * HEADS
    n = HEADS * zs
    nk = 2 * n

    def share(value, shift, back=False):
        step = ys - shift if back else shift
        return lax.ppermute(value, "inner", [(j, (j + step) % ys) for j in range(ys)])

    def cross(value):
        return lax.ppermute(value, "core", [(0, 1), (1, 0)])

    def block_of(x, c, j, k):
        return (((x // xs * 2 + c) * xs + x % xs) * zs + j) * ys + k

    slot = jnp.arange(nq, dtype=jnp.int32)
    q_block = block_of(head ^ (slot % HEADS), core, z, (inner - slot // HEADS) % ys)
    slot = jnp.arange(nk, dtype=jnp.int32)
    k_block = block_of((slot % n) // zs, core ^ (slot // n), slot % zs, inner)
    every = jnp.arange(block_order.shape[0], dtype=jnp.int32)

    def ranked(block):
        pos = jnp.sum(jnp.where(block[:, None] == every[None, :], block_order[None, :], 0), axis=1)
        rank = jnp.sum((pos[None, :] < pos[:, None]).astype(jnp.int32), axis=1)
        n = block.shape[0]
        hit = rank[None, :] == jnp.arange(n, dtype=jnp.int32)[:, None]
        return rank, jnp.sum(jnp.where(hit, pos[None, :], 0), axis=1)

    q_rank, q_sorted = ranked(q_block)
    k_rank, k_sorted = ranked(k_block)
    meta = jnp.concatenate([q_rank, k_rank, q_sorted, k_sorted])
    head_word = head[None].astype(jnp.int32)

    wide, quad = sds((BLK, 2 * G * D), BF), sds((HEADS, BLK, G * D), BF)
    full_in, thin_in = pltpu.VMEM(queries.shape, BF), pltpu.VMEM(keys.shape, BF)
    *sends, kv_send = call(
        pack_body,
        (wide,) * HEADS + (sds((n, BLK, 2 * D), BF),),
        1,
        4,
        [full_in, thin_in, thin_in, full_in, pltpu.SemaphoreType.DMA((4,))],
        space=HBM,
        limit=60 * 1024 * 1024,
    )(head_word, queries, keys, values, grad_out)
    with jax.named_scope("keys_in"):
        kv = lax.all_to_all(kv_send, XAXES + ("z",), split_axis=0, concat_axis=0, tiled=True)

    def spread(mine):
        return [mine] + [share(mine, shift) for shift in shifts[1:]]

    nrow, nkey = nq * BLK * G, nk * BLK
    nt, nj = nq // TB, nk // KB
    tiles = sds((nt, D, ROWS), BF)
    rows = sds((nrow, D), BF)
    key_rows = sds((nkey, D), BF)
    pairs = sds((nt, nkey, ROWS), BF)
    stat = sds((2, nrow), F32)
    work = nrow * nkey
    with jax.named_scope("queries_in"):
        arrived = [sends[0]] + [flip(XAXES, sends[x], x) for x in range(1, HEADS)]
        q_mine, g_mine = call(collect_body, (quad, quad), 0, HEADS)(*arrived)
        q_all = spread(q_mine)
    with jax.named_scope("keys_cross_in"):
        q_all, g_mine, kv = lax.optimization_barrier((q_all, g_mine, kv))
        kv_far = cross(kv)
    with jax.named_scope("queries_in"):
        qn, qt = call(functools.partial(stage_body, cn), (rows, tiles), 1, cn)(meta, *q_all)
    with jax.named_scope("grads_in"):
        g_all = spread(g_mine)
    logs, ot, ks, vs, weights = call(
        functools.partial(forward_body, cn, nk),
        (stat, sds((nt, D, ROWS), F32), key_rows, key_rows, pairs),
        1,
        3,
        forward_scratch(nk),
        pl.CostEstimate(flops=4 * work * D, bytes_accessed=1 << 22, transcendentals=work),
    )(meta, qt, kv, kv_far)
    stats, gt = call(
        functools.partial(delta_body, cn), (stat, tiles), 1, cn + 2, [pltpu.VMEM((nrow, D), BF)]
    )(meta, logs, ot, *g_all)
    with jax.named_scope("stats"):
        all_stats = [stats] + [share(stats, shift) for shift in shifts[1:]]
    with jax.named_scope("attended_out"):
        late_ot, _ = lax.optimization_barrier((ot, stats))
        on = call(attended_body, rows, 0, 1, cost=pl.CostEstimate(flops=0, bytes_accessed=1 << 22, transcendentals=0))(late_ot)
    double = sds((HEADS, BLK, 2 * G * D), BF)
    kv_near, kv_far, *q_parts = call(
        functools.partial(backward_body, cn, nk),
        (sds((n, BLK, 2 * D), BF),) * 2 + (double,) * cn,
        1,
        cn + 7,
        [
            pltpu.VMEM((nkey, D), F32),
            pltpu.VMEM((nkey, D), F32),
            pltpu.VMEM((D, ROWS), F32),
            pltpu.VMEM((nrow, D), BF),
            pltpu.VMEM((ROWS, D), BF),
            pltpu.VMEM((1, nrow), F32),
            pltpu.VMEM((1, nrow), F32),
            pltpu.VMEM((nj, D, TK), BF),
        ],
        pl.CostEstimate(flops=8 * work * D, bytes_accessed=1 << 22, transcendentals=0),
    )(meta, *all_stats, logs, qn, gt, ks, vs, weights, on)
    with jax.named_scope("keys_out"):
        kv_part = call(add_body, sds((n, BLK, 2 * D), BF), 0, 2)(kv_near, cross(kv_far))
        kv_parts = lax.all_to_all(kv_part, XAXES + ("z",), split_axis=0, concat_axis=0, tiled=True)
    opposite = [(ys - shift) % ys for shift in shifts]
    with jax.named_scope("queries_out"):
        back = [q_parts[0]] + [share(part, shift, True) for part, shift in zip(q_parts[1:], shifts[1:])]
        sums = call(
            functools.partial(sum_body, cn), (wide,) * HEADS, 1, 2 * cn, [pltpu.VMEM((nrow, D), F32)]
        )(meta, *[all_stats[i] for i in opposite], *back)
        final = [sums[0]] + [flip(XAXES, sums[x], x) for x in range(1, HEADS)]
        full = sds(queries.shape, BF)
        attended, grad_queries = call(place_body, (full, full), 1, HEADS)(head_word, *final)
    with jax.named_scope("key_sums"):
        thin = sds(keys.shape, BF)
        grad_keys, grad_values = call(key_sum_body, (thin, thin), 0, 1)(kv_parts)
    return attended, grad_queries, grad_keys, grad_values


def solution(mesh):
    heads, outer, inner = (mesh.shape[name] for name in ("head", "outer", "inner"))
    names = ("xhi", "core", "xlo", "z", "inner")
    split = Mesh(mesh.devices.reshape(heads // 2, 2, 2, outer // 2, inner), names)
    rows = P(names, None)
    return jax.shard_map(
        per_device,
        mesh=split,
        in_specs=(rows, rows, rows, rows, P()),
        out_specs=(rows, rows, rows, rows),
        check_vma=False,
    )
```

```python
import functools
import math

import jax
import jax.numpy as jnp
from jax import lax
from jax.experimental import pallas as pl
from jax.experimental.pallas import tpu as pltpu
from jax.sharding import Mesh, PartitionSpec as P

D = 128
BLK = 32
G = 4
HEADS = 4
TB = 4
ROWS = TB * BLK * G
KB = 16
TK = KB * BLK
KBF = 32
TKF = KBF * BLK
SUB = 256
SCALE = 1.0 / math.sqrt(D)
C2 = SCALE * math.log2(math.e)
LOW = -1e30
XAXES = ("xhi", "xlo")
LIMIT = 20 * 1024 * 1024
F32, BF = jnp.float32, jnp.bfloat16
VMEM = pl.BlockSpec(memory_space=pltpu.VMEM)
HBM = pl.BlockSpec(memory_space=pltpu.HBM)
SMEM = pl.BlockSpec(memory_space=pltpu.SMEM)


def mo(value, by):
    return pl.multiple_of(value, by)


def call(body, out_shape, n_smem, n_in, scratch=(), cost=None, space=VMEM, limit=LIMIT):
    return pl.pallas_call(
        body,
        out_shape=out_shape,
        in_specs=[SMEM] * n_smem + [space] * n_in,
        out_specs=jax.tree.map(lambda _: VMEM, out_shape),
        scratch_shapes=list(scratch),
        compiler_params=pltpu.CompilerParams(vmem_limit_bytes=limit),
        cost_estimate=cost,
    )


def sds(shape, dtype):
    return jax.ShapeDtypeStruct(shape, dtype)


def pack_body(head, q_in, k_in, v_in, g_in, *refs):
    sends, kv_out = refs[:HEADS], refs[HEADS]
    q, k, v, g, sems = refs[HEADS + 1 :]
    copies = [
        pltpu.make_async_copy(source, target, sems.at[n])
        for n, (source, target) in enumerate(((k_in, k), (v_in, v), (q_in, q), (g_in, g)))
    ]
    for copy in copies:
        copy.start()
    copies[0].wait()
    copies[1].wait()
    fan = kv_out.shape[0] // HEADS
    for j in range(HEADS):
        both = jnp.concatenate([k[:, j * D : (j + 1) * D], v[:, j * D : (j + 1) * D]], axis=1)
        for f in range(fan):
            kv_out[j * fan + f] = both
    h = head[0]
    copies[2].wait()
    copies[3].wait()
    for x in range(HEADS):
        cols = pl.ds(mo((h ^ x) * (G * D), G * D), G * D)
        sends[x][:, : G * D] = q[:, cols]
        sends[x][:, G * D :] = g[:, cols]


def collect_body(*refs):
    parts, (queries, grads) = refs[:HEADS], refs[HEADS:]
    for x in range(HEADS):
        queries[x] = parts[x][:, : G * D]
        grads[x] = parts[x][:, G * D :]


def tile_bounds(meta, nq, nk, t, kb):
    q_at, k_at = nq + nk, 2 * nq + nk
    first, last = meta[q_at + t * TB], meta[q_at + t * TB + TB - 1]
    full, need = jnp.int32(0), jnp.int32(0)
    for j in range(nk // kb):
        need += (meta[k_at + j * kb] <= last).astype(jnp.int32)
        full += (meta[k_at + j * kb + kb - 1] < first).astype(jnp.int32)
    return full, need


def query_lane(meta, nq, nk, t):
    lane = lax.broadcasted_iota(jnp.int32, (1, ROWS), 1)
    block = (lane // BLK) % TB
    pos = jnp.zeros((1, ROWS), jnp.int32)
    for b in range(TB):
        pos = jnp.where(block == b, meta[nq + nk + t * TB + b], pos)
    return pos * BLK + lane % BLK


def masked_scores(meta, nq, nk, scores, lane_pos, first):
    row = lax.broadcasted_iota(jnp.int32, (BLK, ROWS), 0)
    parts = []
    for b in range(scores.shape[0] // BLK):
        at = meta[2 * nq + nk + first + b] * BLK
        allowed = row <= lane_pos - at
        parts.append(jnp.where(allowed, scores[b * BLK : (b + 1) * BLK], LOW))
    return jnp.concatenate(parts, axis=0)


def dot(a, b):
    return lax.dot_general(a, b, (((1,), (0,)), ((), ())), preferred_element_type=F32)


def row_slots(meta, cn):
    for r in range(cn):
        for x in range(HEADS):
            n = meta[r * HEADS + x]
            yield r, x, (n // TB) * ROWS + (n % TB) * BLK


def rows_at(base, g):
    return pl.ds(mo(base + g * TB * BLK, BLK), BLK)


def stage_body(cn, meta, *refs):
    parts, (rows, tiles) = refs[:cn], refs[cn:]
    for r, x, base in row_slots(meta, cn):
        for g in range(G):
            rows[rows_at(base, g), :] = parts[r][x, :, g * D : (g + 1) * D]
    for t in range(tiles.shape[0]):
        tiles[t] = rows[t * ROWS : (t + 1) * ROWS, :].T


def forward_scratch(nk):
    return [pltpu.VMEM((nk // KBF, D, TKF), BF), pltpu.VMEM((nk * BLK, ROWS), F32)]


def forward_body(cn, nk, meta, qt, kv_near, kv_far, logs, ot, ks, vs, weights_out, vt, sbuf):
    nq = cn * HEADS
    nt, nj = nq // TB, nk // KBF
    for s in range(nk):
        at = pl.ds(mo(meta[nq + s] * BLK, BLK), BLK)
        kv = (kv_near, kv_far)[s // (nk // 2)]
        ks[at, :] = kv[s % (nk // 2), :, :D]
        vs[at, :] = kv[s % (nk // 2), :, D:]
    for j in range(nj):
        vt[j] = vs[j * TKF : (j + 1) * TKF, :].T

    def tile(t, unused):
        full, need = tile_bounds(meta, nq, nk, t, KBF)
        lane_pos = query_lane(meta, nq, nk, t)
        query = qt[t]

        def score(masked, j, run):
            for c in range(TKF // SUB):
                at = pl.ds(mo(j * TKF + c * SUB, SUB), SUB)
                scores = dot(ks[at, :], query)
                if masked:
                    scores = masked_scores(meta, nq, nk, scores, lane_pos, j * KBF + c * (SUB // BLK))
                sbuf[at, :] = scores
                run = jnp.maximum(run, jnp.max(scores, axis=0, keepdims=True))
            return run

        run = jnp.full((1, ROWS), LOW * 0.1, F32)
        run = lax.fori_loop(0, full, functools.partial(score, False), run)
        run = lax.fori_loop(full, need, functools.partial(score, True), run)
        top = run * C2

        def step(j, state):
            total, acc = state
            for c in range(TKF // SUB):
                at = pl.ds(mo(j * TKF + c * SUB, SUB), SUB)
                weights = jnp.exp2(sbuf[at, :] * C2 - top)
                total += jnp.sum(weights, axis=0, keepdims=True)
                rounded = weights.astype(BF)
                weights_out[t, at, :] = rounded
                acc += dot(vt[j, :, c * SUB : (c + 1) * SUB], rounded)
            return total, acc

        state = (jnp.zeros((1, ROWS), F32), jnp.zeros((D, ROWS), F32))
        total, acc = lax.fori_loop(0, need, step, state)
        some = total > 0.0
        safe = jnp.where(some, total, 1.0)
        lanes = pl.ds(mo(t * ROWS, ROWS), ROWS)
        logs[0:1, lanes] = jnp.where(some, top + jnp.log2(safe), LOW)
        logs[1:2, lanes] = top
        ot[t] = acc * jnp.where(some, 1.0 / safe, 0.0)
        return unused

    lax.fori_loop(0, nt, tile, 0)


def delta_body(cn, meta, logs, ot, *refs):
    parts, (stats, gt, gn) = refs[:cn], refs[cn:]
    for r, x, base in row_slots(meta, cn):
        for g in range(G):
            gn[rows_at(base, g), :] = parts[r][x, :, g * D : (g + 1) * D]
    stats[0:1, :] = logs[0:1, :]
    for t in range(gt.shape[0]):
        lanes = slice(t * ROWS, (t + 1) * ROWS)
        grads = gn[lanes, :].T
        gt[t] = grads
        stats[1:2, lanes] = jnp.sum(ot[t] * grads.astype(F32), axis=0, keepdims=True)


def attended_body(cn, meta, ot, ks, *refs):
    outs, kt, on = refs[:cn], refs[cn], refs[cn + 1]
    for t in range(ot.shape[0]):
        on[t * ROWS : (t + 1) * ROWS, :] = ot[t].astype(BF).T
    for r, x, base in row_slots(meta, cn):
        for g in range(G):
            outs[r][x, :, g * D : (g + 1) * D] = on[rows_at(base, g), :]
    for j in range(kt.shape[0]):
        kt[j] = ks[j * TK : (j + 1) * TK, :].T


def combine(stats):
    logs = [s[0:1, :] for s in stats]
    top = functools.reduce(jnp.maximum, logs)
    parts = [jnp.exp2(log - top) for log in logs]
    whole = functools.reduce(jnp.add, parts)
    return parts, whole, top


def backward_body(cn, nk, meta, *refs):
    stats = refs[:cn]
    logs, qn, gt, kt, vs, weights = refs[cn : cn + 6]
    near, far, *outs = refs[cn + 6 : 2 * cn + 8]
    dk, dv, dqt, dqn, gn, scale_all, delta_all = refs[2 * cn + 8 :]
    nq = cn * HEADS
    nt = nq // TB

    parts, whole, top = combine(stats)
    scale_all[...] = jnp.exp2(logs[1:2, :] - top) / whole
    delta_all[...] = functools.reduce(jnp.add, [p * s[1:2, :] for p, s in zip(parts, stats)]) / whole
    dk[...] = jnp.zeros_like(dk)
    dv[...] = jnp.zeros_like(dv)

    def tile(t, unused):
        full, need = tile_bounds(meta, nq, nk, t, KB)
        lanes = pl.ds(mo(t * ROWS, ROWS), ROWS)
        scale, delta = scale_all[:, lanes], delta_all[:, lanes]
        gn[...] = (gt[t].astype(F32) * scale).astype(BF).T
        dqt[...] = jnp.zeros_like(dqt)

        def step(j, state):
            for c in range(TK // SUB):
                keys = pl.ds(mo(j * TK + c * SUB, SUB), SUB)
                own = weights[t, keys, :]
                lean = (dot(vs[keys, :], gt[t]) - delta) * scale
                grad_scores = (own.astype(F32) * lean).astype(BF)
                dv[keys, :] += dot(own, gn[...])
                dk[keys, :] += dot(grad_scores, qn[lanes, :])
                dqt[...] += dot(kt[j, :, c * SUB : (c + 1) * SUB], grad_scores)
            return state

        lax.fori_loop(0, need, step, 0)
        dqn[lanes, :] = (dqt[...] * SCALE).astype(BF).T
        return unused

    lax.fori_loop(0, nt, tile, 0)
    for s in range(nk):
        at = pl.ds(mo(meta[nq + s] * BLK, BLK), BLK)
        kv_out = (near, far)[s // (nk // 2)]
        kv_out[s % (nk // 2), :, :D] = (dk[at, :] * SCALE).astype(BF)
        kv_out[s % (nk // 2), :, D:] = dv[at, :].astype(BF)
    for r, x, base in row_slots(meta, cn):
        for g in range(G):
            outs[r][x, :, g * D : (g + 1) * D] = dqn[rows_at(base, g), :]


def add_body(one, two, out):
    out[...] = (one[...].astype(F32) + two[...].astype(F32)).astype(BF)


def sum_body(cn, meta, *refs):
    stats, attended, grads = refs[:cn], refs[cn : 2 * cn], refs[2 * cn : 3 * cn]
    outs, columns = refs[3 * cn : 3 * cn + HEADS], refs[3 * cn + HEADS]
    parts, whole, top = combine(stats)
    inverse = 1.0 / whole
    spread = D // cn
    tall = jnp.concatenate([jnp.broadcast_to(p * inverse, (spread, p.shape[1])) for p in parts], axis=0)
    for t in range(tall.shape[1] // ROWS):
        columns[t * ROWS : (t + 1) * ROWS, :] = tall[:, t * ROWS : (t + 1) * ROWS].T
    for r, x, base in row_slots(meta, 1):
        for g in range(G):
            cols = slice(g * D, (g + 1) * D)
            column = columns[rows_at(base, g), :]
            total = jnp.zeros((BLK, D), F32)
            for i in range(cn):
                total += column[:, i * spread : i * spread + 1] * attended[i][x, :, cols].astype(F32)
            outs[x][:, cols] = total.astype(BF)
        total = grads[0][x].astype(F32)
        for i in range(1, cn):
            total += grads[i][x].astype(F32)
        outs[x][:, G * D :] = total.astype(BF)


def place_body(head, *refs):
    parts, attended, grad = refs[:HEADS], refs[HEADS], refs[HEADS + 1]
    h = head[0]
    for x in range(HEADS):
        cols = pl.ds(mo((h ^ x) * (G * D), G * D), G * D)
        attended[:, cols] = parts[x][:, : G * D]
        grad[:, cols] = parts[x][:, G * D :]


def key_sum_body(parts, dk, dv):
    fan = parts.shape[0] // HEADS
    for j in range(HEADS):
        total = parts[j * fan].astype(F32)
        for f in range(1, fan):
            total += parts[j * fan + f].astype(F32)
        dk[:, j * D : (j + 1) * D] = total[:, :D].astype(BF)
        dv[:, j * D : (j + 1) * D] = total[:, D:].astype(BF)


def flip(axis, value, x):
    return lax.ppermute(value, axis, [(j, j ^ x) for j in range(HEADS)])


def per_device(queries, keys, values, grad_out, block_order):
    xs, zs, ys = lax.axis_size("xlo"), lax.axis_size("z"), lax.axis_size("inner")
    head, core = lax.axis_index(XAXES), lax.axis_index("core")
    z, inner = lax.axis_index("z"), lax.axis_index("inner")
    shifts = range(ys)
    cn = ys
    nq = cn * HEADS
    n = HEADS * zs
    nk = 2 * n

    def share(value, shift, back=False):
        step = ys - shift if back else shift
        return lax.ppermute(value, "inner", [(j, (j + step) % ys) for j in range(ys)])

    def cross(value):
        return lax.ppermute(value, "core", [(0, 1), (1, 0)])

    def block_of(x, c, j, k):
        return (((x // xs * 2 + c) * xs + x % xs) * zs + j) * ys + k

    slot = jnp.arange(nq, dtype=jnp.int32)
    q_block = block_of(head ^ (slot % HEADS), core, z, (inner - slot // HEADS) % ys)
    slot = jnp.arange(nk, dtype=jnp.int32)
    k_block = block_of((slot % n) // zs, core ^ (slot // n), slot % zs, inner)
    every = jnp.arange(block_order.shape[0], dtype=jnp.int32)

    def ranked(block):
        pos = jnp.sum(jnp.where(block[:, None] == every[None, :], block_order[None, :], 0), axis=1)
        rank = jnp.sum((pos[None, :] < pos[:, None]).astype(jnp.int32), axis=1)
        n = block.shape[0]
        hit = rank[None, :] == jnp.arange(n, dtype=jnp.int32)[:, None]
        return rank, jnp.sum(jnp.where(hit, pos[None, :], 0), axis=1)

    q_rank, q_sorted = ranked(q_block)
    k_rank, k_sorted = ranked(k_block)
    meta = jnp.concatenate([q_rank, k_rank, q_sorted, k_sorted])
    head_word = head[None].astype(jnp.int32)

    wide, quad = sds((BLK, 2 * G * D), BF), sds((HEADS, BLK, G * D), BF)
    full_in, thin_in = pltpu.VMEM(queries.shape, BF), pltpu.VMEM(keys.shape, BF)
    *sends, kv_send = call(
        pack_body,
        (wide,) * HEADS + (sds((n, BLK, 2 * D), BF),),
        1,
        4,
        [full_in, thin_in, thin_in, full_in, pltpu.SemaphoreType.DMA((4,))],
        space=HBM,
        limit=60 * 1024 * 1024,
    )(head_word, queries, keys, values, grad_out)
    with jax.named_scope("keys_in"):
        kv = lax.all_to_all(kv_send, XAXES + ("z",), split_axis=0, concat_axis=0, tiled=True)

    def spread(mine):
        return [mine] + [share(mine, shift) for shift in shifts[1:]]

    nrow, nkey = nq * BLK * G, nk * BLK
    nt, nj = nq // TB, nk // KB
    tiles = sds((nt, D, ROWS), BF)
    rows = sds((nrow, D), BF)
    key_rows = sds((nkey, D), BF)
    pairs = sds((nt, nkey, ROWS), BF)
    stat = sds((2, nrow), F32)
    work = nrow * nkey
    with jax.named_scope("queries_in"):
        arrived = [sends[0]] + [flip(XAXES, sends[x], x) for x in range(1, HEADS)]
        q_mine, g_mine = call(collect_body, (quad, quad), 0, HEADS)(*arrived)
        q_all = spread(q_mine)
    with jax.named_scope("keys_cross_in"):
        q_all, g_mine, kv = lax.optimization_barrier((q_all, g_mine, kv))
        kv_far = cross(kv)
    with jax.named_scope("queries_in"):
        qn, qt = call(functools.partial(stage_body, cn), (rows, tiles), 1, cn)(meta, *q_all)
    with jax.named_scope("grads_in"):
        g_all = spread(g_mine)
    logs, ot, ks, vs, weights = call(
        functools.partial(forward_body, cn, nk),
        (stat, sds((nt, D, ROWS), F32), key_rows, key_rows, pairs),
        1,
        3,
        forward_scratch(nk),
        pl.CostEstimate(flops=4 * work * D, bytes_accessed=1 << 22, transcendentals=work),
    )(meta, qt, kv, kv_far)
    stats, gt = call(
        functools.partial(delta_body, cn), (stat, tiles), 1, cn + 2, [pltpu.VMEM((nrow, D), BF)]
    )(meta, logs, ot, *g_all)
    with jax.named_scope("stats"):
        all_stats = [stats] + [share(stats, shift) for shift in shifts[1:]]
    with jax.named_scope("attended_out"):
        late_ot, _ = lax.optimization_barrier((ot, stats))
        *o_parts, kt = call(
            functools.partial(attended_body, cn),
            (quad,) * cn + (sds((nj, D, TK), BF),),
            1,
            2,
            [pltpu.VMEM((nrow, D), BF)],
            pl.CostEstimate(flops=0, bytes_accessed=1 << 22, transcendentals=0),
        )(meta, late_ot, ks)
        o_back = [o_parts[0]] + [share(part, shift, True) for part, shift in zip(o_parts[1:], shifts[1:])]
    kv_near, kv_far, *q_parts = call(
        functools.partial(backward_body, cn, nk),
        (sds((n, BLK, 2 * D), BF),) * 2 + (quad,) * cn,
        1,
        cn + 6,
        [
            pltpu.VMEM((nkey, D), F32),
            pltpu.VMEM((nkey, D), F32),
            pltpu.VMEM((D, ROWS), F32),
            pltpu.VMEM((nrow, D), BF),
            pltpu.VMEM((ROWS, D), BF),
            pltpu.VMEM((1, nrow), F32),
            pltpu.VMEM((1, nrow), F32),
        ],
        pl.CostEstimate(flops=8 * work * D, bytes_accessed=1 << 22, transcendentals=0),
    )(meta, *all_stats, logs, qn, gt, kt, vs, weights)
    with jax.named_scope("keys_out"):
        kv_near, kv_far, q_parts, o_back = lax.optimization_barrier((kv_near, kv_far, q_parts, o_back))
        kv_part = call(add_body, sds((n, BLK, 2 * D), BF), 0, 2)(kv_near, cross(kv_far))
        kv_parts = lax.all_to_all(kv_part, XAXES + ("z",), split_axis=0, concat_axis=0, tiled=True)
    opposite = [(ys - shift) % ys for shift in shifts]
    with jax.named_scope("queries_out"):
        back = [q_parts[0]] + [share(part, shift, True) for part, shift in zip(q_parts[1:], shifts[1:])]
        sums = call(
            functools.partial(sum_body, cn), (wide,) * HEADS, 1, 3 * cn, [pltpu.VMEM((nrow, D), F32)]
        )(meta, *[all_stats[i] for i in opposite], *o_back, *back)
        final = [sums[0]] + [flip(XAXES, sums[x], x) for x in range(1, HEADS)]
        full = sds(queries.shape, BF)
        attended, grad_queries = call(place_body, (full, full), 1, HEADS)(head_word, *final)
    with jax.named_scope("key_sums"):
        thin = sds(keys.shape, BF)
        grad_keys, grad_values = call(key_sum_body, (thin, thin), 0, 1)(kv_parts)
    return attended, grad_queries, grad_keys, grad_values


def solution(mesh):
    heads, outer, inner = (mesh.shape[name] for name in ("head", "outer", "inner"))
    names = ("xhi", "core", "xlo", "z", "inner")
    split = Mesh(mesh.devices.reshape(heads // 2, 2, 2, outer // 2, inner), names)
    rows = P(names, None)
    return jax.shard_map(
        per_device,
        mesh=split,
        in_specs=(rows, rows, rows, rows, P()),
        out_specs=(rows, rows, rows, rows),
        check_vma=False,
    )
```

```python
import functools
import math

import jax
import jax.numpy as jnp
from jax import lax
from jax.experimental import pallas as pl
from jax.experimental.pallas import tpu as pltpu
from jax.sharding import Mesh, PartitionSpec as P

D = 128
BLK = 32
G = 4
HEADS = 4
TB = 4
ROWS = TB * BLK * G
KB = 16
TK = KB * BLK
SUB = 256
SCALE = 1.0 / math.sqrt(D)
C2 = SCALE * math.log2(math.e)
LOW = -1e30
XAXES = ("xhi", "xlo")
LIMIT = 20 * 1024 * 1024
F32, BF = jnp.float32, jnp.bfloat16
VMEM = pl.BlockSpec(memory_space=pltpu.VMEM)
HBM = pl.BlockSpec(memory_space=pltpu.HBM)
SMEM = pl.BlockSpec(memory_space=pltpu.SMEM)


def mo(value, by):
    return pl.multiple_of(value, by)


def call(body, out_shape, n_smem, n_in, scratch=(), cost=None, space=VMEM, limit=LIMIT):
    return pl.pallas_call(
        body,
        out_shape=out_shape,
        in_specs=[SMEM] * n_smem + [space] * n_in,
        out_specs=jax.tree.map(lambda _: VMEM, out_shape),
        scratch_shapes=list(scratch),
        compiler_params=pltpu.CompilerParams(vmem_limit_bytes=limit),
        cost_estimate=cost,
    )


def sds(shape, dtype):
    return jax.ShapeDtypeStruct(shape, dtype)


def pack_body(head, q_in, k_in, v_in, g_in, *refs):
    sends, kv_out = refs[:HEADS], refs[HEADS]
    q, k, v, g, sems = refs[HEADS + 1 :]
    copies = [
        pltpu.make_async_copy(source, target, sems.at[n])
        for n, (source, target) in enumerate(((k_in, k), (v_in, v), (q_in, q), (g_in, g)))
    ]
    for copy in copies:
        copy.start()
    copies[0].wait()
    copies[1].wait()
    fan = kv_out.shape[0] // HEADS
    for j in range(HEADS):
        both = jnp.concatenate([k[:, j * D : (j + 1) * D], v[:, j * D : (j + 1) * D]], axis=1)
        for f in range(fan):
            kv_out[j * fan + f] = both
    h = head[0]
    copies[2].wait()
    copies[3].wait()
    for x in range(HEADS):
        cols = pl.ds(mo((h ^ x) * (G * D), G * D), G * D)
        sends[x][:, : G * D] = q[:, cols]
        sends[x][:, G * D :] = g[:, cols]


def collect_body(*refs):
    parts, (queries, grads) = refs[:HEADS], refs[HEADS:]
    for x in range(HEADS):
        queries[x] = parts[x][:, : G * D]
        grads[x] = parts[x][:, G * D :]


def tiles_needed(meta, nq, nk, t, kb):
    last = meta[nq + nk + t * TB + TB - 1]
    need = jnp.int32(0)
    for j in range(nk // kb):
        need += (meta[2 * nq + nk + j * kb] <= last).astype(jnp.int32)
    return need


def in_pairs(need, step, width, state):
    state = lax.fori_loop(0, need // 2, functools.partial(step, 2 * width), state)
    return lax.fori_loop(need // 2 * 2, need, functools.partial(step, width), state)


def query_lane(meta, nq, nk, t):
    lane = lax.broadcasted_iota(jnp.int32, (1, ROWS), 1)
    block = (lane // BLK) % TB
    pos = jnp.zeros((1, ROWS), jnp.int32)
    for b in range(TB):
        pos = jnp.where(block == b, meta[nq + nk + t * TB + b], pos)
    return pos * BLK + lane % BLK


def masked_scores(meta, nq, nk, scores, lane_pos, first):
    row = lax.broadcasted_iota(jnp.int32, (BLK, ROWS), 0)
    parts = []
    for b in range(scores.shape[0] // BLK):
        at = meta[2 * nq + nk + first + b] * BLK
        allowed = row <= lane_pos - at
        parts.append(jnp.where(allowed, scores[b * BLK : (b + 1) * BLK], LOW))
    return jnp.concatenate(parts, axis=0)


def dot(a, b):
    return lax.dot_general(a, b, (((1,), (0,)), ((), ())), preferred_element_type=F32)


def row_slots(meta, cn):
    for r in range(cn):
        for x in range(HEADS):
            n = meta[r * HEADS + x]
            yield r, x, (n // TB) * ROWS + (n % TB) * BLK


def rows_at(base, g):
    return pl.ds(mo(base + g * TB * BLK, BLK), BLK)


def stage_body(cn, meta, *refs):
    parts, (rows, tiles) = refs[:cn], refs[cn:]
    for r, x, base in row_slots(meta, cn):
        for g in range(G):
            rows[rows_at(base, g), :] = parts[r][x, :, g * D : (g + 1) * D]
    for t in range(tiles.shape[0]):
        tiles[t] = rows[t * ROWS : (t + 1) * ROWS, :].T


def stage_keys_body(nq, nk, meta, kv_near, kv_far, ks, vs, vt):
    for s in range(nk):
        at = pl.ds(mo(meta[nq + s] * BLK, BLK), BLK)
        kv = (kv_near, kv_far)[s // (nk // 2)]
        ks[at, :] = kv[s % (nk // 2), :, :D]
        vs[at, :] = kv[s % (nk // 2), :, D:]
    for j in range(vt.shape[0]):
        vt[j] = vs[j * TK : (j + 1) * TK, :].T


def forward_body(nq, nk, meta, qt, ks, vt, logs, ot, weights_out, sbuf):
    def tile(t, unused):
        need = tiles_needed(meta, nq, nk, t, KB)
        lane_pos = query_lane(meta, nq, nk, t)
        query = qt[t]

        def score(width, j, run):
            for c in range(0, width, SUB):
                at = pl.ds(mo(j * width + c, SUB), SUB)
                scores = dot(ks[at, :], query)
                scores = masked_scores(meta, nq, nk, scores, lane_pos, (j * width + c) // BLK)
                sbuf[at, :] = scores
                run = jnp.maximum(run, jnp.max(scores, axis=0, keepdims=True))
            return run

        top = in_pairs(need, score, TK, jnp.full((1, ROWS), LOW * 0.1, F32)) * C2

        def step(width, j, state):
            total, acc = state
            for c in range(0, width, SUB):
                at = pl.ds(mo(j * width + c, SUB), SUB)
                weights = jnp.exp2(sbuf[at, :] * C2 - top)
                total += jnp.sum(weights, axis=0, keepdims=True)
                rounded = weights.astype(BF)
                weights_out[t, at, :] = rounded
                acc += dot(vt[j * (width // TK) + c // TK, :, c % TK : c % TK + SUB], rounded)
            return total, acc

        state = (jnp.zeros((1, ROWS), F32), jnp.zeros((D, ROWS), F32))
        total, acc = in_pairs(need, step, TK, state)
        some = total > 0.0
        safe = jnp.where(some, total, 1.0)
        lanes = pl.ds(mo(t * ROWS, ROWS), ROWS)
        logs[0:1, lanes] = jnp.where(some, top + jnp.log2(safe), LOW)
        logs[1:2, lanes] = top
        ot[t] = acc * jnp.where(some, 1.0 / safe, 0.0)
        return unused

    lax.fori_loop(0, nq // TB, tile, 0)


def delta_body(cn, meta, logs, ot, *refs):
    parts, (stats, gt, gn) = refs[:cn], refs[cn:]
    for r, x, base in row_slots(meta, cn):
        for g in range(G):
            gn[rows_at(base, g), :] = parts[r][x, :, g * D : (g + 1) * D]
    stats[0:1, :] = logs[0:1, :]
    for t in range(gt.shape[0]):
        lanes = slice(t * ROWS, (t + 1) * ROWS)
        grads = gn[lanes, :].T
        gt[t] = grads
        stats[1:2, lanes] = jnp.sum(ot[t] * grads.astype(F32), axis=0, keepdims=True)


def attended_body(cn, meta, ot, ks, *refs):
    outs, kt, on = refs[:cn], refs[cn], refs[cn + 1]
    for t in range(ot.shape[0]):
        on[t * ROWS : (t + 1) * ROWS, :] = ot[t].astype(BF).T
    for r, x, base in row_slots(meta, cn):
        for g in range(G):
            outs[r][x, :, g * D : (g + 1) * D] = on[rows_at(base, g), :]
    for j in range(kt.shape[0]):
        kt[j] = ks[j * TK : (j + 1) * TK, :].T


def combine(stats):
    logs = [s[0:1, :] for s in stats]
    top = functools.reduce(jnp.maximum, logs)
    parts = [jnp.exp2(log - top) for log in logs]
    whole = functools.reduce(jnp.add, parts)
    return parts, whole, top


def backward_body(cn, nk, meta, *refs):
    stats = refs[:cn]
    logs, qn, gt, kt, vs, weights = refs[cn : cn + 6]
    near, far, *outs = refs[cn + 6 : 2 * cn + 8]
    dk, dv, dqt, dqn, gn, scale_all, delta_all = refs[2 * cn + 8 :]
    nq = cn * HEADS
    nt = nq // TB

    parts, whole, top = combine(stats)
    scale_all[...] = jnp.exp2(logs[1:2, :] - top) / whole
    delta_all[...] = functools.reduce(jnp.add, [p * s[1:2, :] for p, s in zip(parts, stats)]) / whole
    dk[...] = jnp.zeros_like(dk)
    dv[...] = jnp.zeros_like(dv)

    def tile(t, unused):
        need = tiles_needed(meta, nq, nk, t, SUB // BLK)
        lanes = pl.ds(mo(t * ROWS, ROWS), ROWS)
        scale, delta = scale_all[:, lanes], delta_all[:, lanes]
        gn[...] = (gt[t].astype(F32) * scale).astype(BF).T
        dqt[...] = jnp.zeros_like(dqt)

        def step(width, j, state):
            for c in range(0, width, SUB):
                keys = pl.ds(mo(j * width + c, SUB), SUB)
                own = weights[t, keys, :]
                lean = (dot(vs[keys, :], gt[t]) - delta) * scale
                grad_scores = (own.astype(F32) * lean).astype(BF)
                dv[keys, :] += dot(own, gn[...])
                dk[keys, :] += dot(grad_scores, qn[lanes, :])
                dqt[...] += dot(kt[j * width // TK, :, c : c + SUB], grad_scores)
            return state

        in_pairs(need, step, SUB, 0)
        dqn[lanes, :] = (dqt[...] * SCALE).astype(BF).T
        return unused

    lax.fori_loop(0, nt, tile, 0)
    for s in range(nk):
        at = pl.ds(mo(meta[nq + s] * BLK, BLK), BLK)
        kv_out = (near, far)[s // (nk // 2)]
        kv_out[s % (nk // 2), :, :D] = (dk[at, :] * SCALE).astype(BF)
        kv_out[s % (nk // 2), :, D:] = dv[at, :].astype(BF)
    for r, x, base in row_slots(meta, cn):
        for g in range(G):
            outs[r][x, :, g * D : (g + 1) * D] = dqn[rows_at(base, g), :]


def add_body(one, two, out):
    out[...] = (one[...].astype(F32) + two[...].astype(F32)).astype(BF)


def sum_body(cn, meta, *refs):
    stats, attended, grads = refs[:cn], refs[cn : 2 * cn], refs[2 * cn : 3 * cn]
    outs, columns = refs[3 * cn : 3 * cn + HEADS], refs[3 * cn + HEADS]
    parts, whole, top = combine(stats)
    inverse = 1.0 / whole
    spread = D // cn
    tall = jnp.concatenate([jnp.broadcast_to(p * inverse, (spread, p.shape[1])) for p in parts], axis=0)
    for t in range(tall.shape[1] // ROWS):
        columns[t * ROWS : (t + 1) * ROWS, :] = tall[:, t * ROWS : (t + 1) * ROWS].T
    for r, x, base in row_slots(meta, 1):
        for g in range(G):
            cols = slice(g * D, (g + 1) * D)
            column = columns[rows_at(base, g), :]
            total = jnp.zeros((BLK, D), F32)
            for i in range(cn):
                total += column[:, i * spread : i * spread + 1] * attended[i][x, :, cols].astype(F32)
            outs[x][:, cols] = total.astype(BF)
        total = grads[0][x].astype(F32)
        for i in range(1, cn):
            total += grads[i][x].astype(F32)
        outs[x][:, G * D :] = total.astype(BF)


def place_body(head, *refs):
    parts, shares = refs[:HEADS], refs[HEADS]
    attended, grad, dk, dv = refs[HEADS + 1 :]
    h = head[0]
    for x in range(HEADS):
        cols = pl.ds(mo((h ^ x) * (G * D), G * D), G * D)
        attended[:, cols] = parts[x][:, : G * D]
        grad[:, cols] = parts[x][:, G * D :]
    fan = shares.shape[0] // HEADS
    for j in range(HEADS):
        total = shares[j * fan].astype(F32)
        for f in range(1, fan):
            total += shares[j * fan + f].astype(F32)
        dk[:, j * D : (j + 1) * D] = total[:, :D].astype(BF)
        dv[:, j * D : (j + 1) * D] = total[:, D:].astype(BF)


def flip(axis, value, x):
    return lax.ppermute(value, axis, [(j, j ^ x) for j in range(HEADS)])


def per_device(queries, keys, values, grad_out, block_order):
    xs, zs, ys = lax.axis_size("xlo"), lax.axis_size("z"), lax.axis_size("inner")
    head, core = lax.axis_index(XAXES), lax.axis_index("core")
    z, inner = lax.axis_index("z"), lax.axis_index("inner")
    shifts = range(ys)
    cn = ys
    nq = cn * HEADS
    n = HEADS * zs
    nk = 2 * n

    def share(value, shift, back=False):
        step = ys - shift if back else shift
        return lax.ppermute(value, "inner", [(j, (j + step) % ys) for j in range(ys)])

    def cross(value):
        return lax.ppermute(value, "core", [(0, 1), (1, 0)])

    def block_of(x, c, j, k):
        return (((x // xs * 2 + c) * xs + x % xs) * zs + j) * ys + k

    slot = jnp.arange(nq, dtype=jnp.int32)
    q_block = block_of(head ^ (slot % HEADS), core, z, (inner - slot // HEADS) % ys)
    slot = jnp.arange(nk, dtype=jnp.int32)
    k_block = block_of((slot % n) // zs, core ^ (slot // n), slot % zs, inner)
    every = jnp.arange(block_order.shape[0], dtype=jnp.int32)

    def ranked(block):
        pos = jnp.sum(jnp.where(block[:, None] == every[None, :], block_order[None, :], 0), axis=1)
        rank = jnp.sum((pos[None, :] < pos[:, None]).astype(jnp.int32), axis=1)
        n = block.shape[0]
        hit = rank[None, :] == jnp.arange(n, dtype=jnp.int32)[:, None]
        return rank, jnp.sum(jnp.where(hit, pos[None, :], 0), axis=1)

    q_rank, q_sorted = ranked(q_block)
    k_rank, k_sorted = ranked(k_block)
    meta = jnp.concatenate([q_rank, k_rank, q_sorted, k_sorted])
    head_word = head[None].astype(jnp.int32)

    wide, quad = sds((BLK, 2 * G * D), BF), sds((HEADS, BLK, G * D), BF)
    full_in, thin_in = pltpu.VMEM(queries.shape, BF), pltpu.VMEM(keys.shape, BF)
    *sends, kv_send = call(
        pack_body,
        (wide,) * HEADS + (sds((n, BLK, 2 * D), BF),),
        1,
        4,
        [full_in, thin_in, thin_in, full_in, pltpu.SemaphoreType.DMA((4,))],
        space=HBM,
        limit=60 * 1024 * 1024,
    )(head_word, queries, keys, values, grad_out)
    with jax.named_scope("keys_in"):
        kv = lax.all_to_all(kv_send, XAXES + ("z",), split_axis=0, concat_axis=0, tiled=True)

    def spread(mine):
        return [mine] + [share(mine, shift) for shift in shifts[1:]]

    nrow, nkey = nq * BLK * G, nk * BLK
    nt, nj = nq // TB, nk // KB
    tiles = sds((nt, D, ROWS), BF)
    rows = sds((nrow, D), BF)
    key_rows = sds((nkey, D), BF)
    pairs = sds((nt, nkey, ROWS), BF)
    stat = sds((2, nrow), F32)
    work = nrow * nkey
    with jax.named_scope("queries_in"):
        arrived = [sends[0]] + [flip(XAXES, sends[x], x) for x in range(1, HEADS)]
        q_mine, g_mine = call(collect_body, (quad, quad), 0, HEADS)(*arrived)
        q_all = spread(q_mine)
    with jax.named_scope("keys_cross_in"):
        kv, q_all = lax.optimization_barrier((kv, q_all))
        ks, vs, vt = call(
            functools.partial(stage_keys_body, nq, nk), (key_rows, key_rows, sds((nj, D, TK), BF)), 1, 2
        )(meta, kv, cross(kv))
    with jax.named_scope("queries_in"):
        q_all, g_mine, ks = lax.optimization_barrier((q_all, g_mine, ks))
        qn, qt = call(functools.partial(stage_body, cn), (rows, tiles), 1, cn)(meta, *q_all)
    with jax.named_scope("grads_in"):
        g_all = spread(g_mine)
    logs, ot, weights = call(
        functools.partial(forward_body, nq, nk),
        (stat, sds((nt, D, ROWS), F32), pairs),
        1,
        3,
        [pltpu.VMEM((nkey, ROWS), F32)],
        pl.CostEstimate(flops=4 * work * D, bytes_accessed=1 << 22, transcendentals=work),
    )(meta, qt, ks, vt)
    stats, gt = call(
        functools.partial(delta_body, cn), (stat, tiles), 1, cn + 2, [pltpu.VMEM((nrow, D), BF)]
    )(meta, logs, ot, *g_all)
    with jax.named_scope("stats"):
        all_stats = [stats] + [share(stats, shift) for shift in shifts[1:]]
    with jax.named_scope("attended_out"):
        late_ot, _ = lax.optimization_barrier((ot, stats))
        *o_parts, kt = call(
            functools.partial(attended_body, cn),
            (quad,) * cn + (sds((nj, D, TK), BF),),
            1,
            2,
            [pltpu.VMEM((nrow, D), BF)],
            pl.CostEstimate(flops=0, bytes_accessed=1 << 22, transcendentals=0),
        )(meta, late_ot, ks)
        o_back = [o_parts[0]] + [share(part, shift, True) for part, shift in zip(o_parts[1:], shifts[1:])]
    kv_near, kv_far, *q_parts = call(
        functools.partial(backward_body, cn, nk),
        (sds((n, BLK, 2 * D), BF),) * 2 + (quad,) * cn,
        1,
        cn + 6,
        [
            pltpu.VMEM((nkey, D), F32),
            pltpu.VMEM((nkey, D), F32),
            pltpu.VMEM((D, ROWS), F32),
            pltpu.VMEM((nrow, D), BF),
            pltpu.VMEM((ROWS, D), BF),
            pltpu.VMEM((1, nrow), F32),
            pltpu.VMEM((1, nrow), F32),
        ],
        pl.CostEstimate(flops=8 * work * D, bytes_accessed=1 << 22, transcendentals=0),
    )(meta, *all_stats, logs, qn, gt, kt, vs, weights)
    with jax.named_scope("keys_out"):
        kv_near, kv_far, q_parts, o_back = lax.optimization_barrier((kv_near, kv_far, q_parts, o_back))
        kv_part = call(add_body, sds((n, BLK, 2 * D), BF), 0, 2)(kv_near, cross(kv_far))
        kv_parts = lax.all_to_all(kv_part, XAXES + ("z",), split_axis=0, concat_axis=0, tiled=True)
    opposite = [(ys - shift) % ys for shift in shifts]
    with jax.named_scope("queries_out"):
        back = [q_parts[0]] + [share(part, shift, True) for part, shift in zip(q_parts[1:], shifts[1:])]
        sums = call(
            functools.partial(sum_body, cn), (wide,) * HEADS, 1, 3 * cn, [pltpu.VMEM((nrow, D), F32)]
        )(meta, *[all_stats[i] for i in opposite], *o_back, *back)
        final = [sums[0]] + [flip(XAXES, sums[x], x) for x in range(1, HEADS)]
    full, thin = sds(queries.shape, BF), sds(keys.shape, BF)
    return call(place_body, (full, full, thin, thin), 1, HEADS + 1)(head_word, *final, kv_parts)


def solution(mesh):
    heads, outer, inner = (mesh.shape[name] for name in ("head", "outer", "inner"))
    names = ("xhi", "core", "xlo", "z", "inner")
    split = Mesh(mesh.devices.reshape(heads // 2, 2, 2, outer // 2, inner), names)
    rows = P(names, None)
    return jax.shard_map(
        per_device,
        mesh=split,
        in_specs=(rows, rows, rows, rows, P()),
        out_specs=(rows, rows, rows, rows),
        check_vma=False,
    )
```

```python
import functools
import math

import jax
import jax.numpy as jnp
from jax import lax
from jax.experimental import pallas as pl
from jax.experimental.pallas import tpu as pltpu
from jax.sharding import Mesh, PartitionSpec as P

D = 128
BLK = 32
G = 4
HEADS = 4
TB = 4
ROWS = TB * BLK * G
KB = 16
TK = KB * BLK
SUB = 256
SCALE = 1.0 / math.sqrt(D)
C2 = SCALE * math.log2(math.e)
LOW = -1e30
XAXES = ("xhi", "xlo")
LIMIT = 20 * 1024 * 1024
F32, BF = jnp.float32, jnp.bfloat16
VMEM = pl.BlockSpec(memory_space=pltpu.VMEM)
HBM = pl.BlockSpec(memory_space=pltpu.HBM)
SMEM = pl.BlockSpec(memory_space=pltpu.SMEM)


def mo(value, by):
    return pl.multiple_of(value, by)


def call(body, out_shape, n_smem, n_in, scratch=(), cost=None, space=VMEM, limit=LIMIT):
    return pl.pallas_call(
        body,
        out_shape=out_shape,
        in_specs=[SMEM] * n_smem + [space] * n_in,
        out_specs=jax.tree.map(lambda _: VMEM, out_shape),
        scratch_shapes=list(scratch),
        compiler_params=pltpu.CompilerParams(vmem_limit_bytes=limit),
        cost_estimate=cost,
    )


def sds(shape, dtype):
    return jax.ShapeDtypeStruct(shape, dtype)


def pack_body(head, q_in, k_in, v_in, g_in, *refs):
    sends, kv_out = refs[:HEADS], refs[HEADS]
    q, k, v, g, sems = refs[HEADS + 1 :]
    copies = [
        pltpu.make_async_copy(source, target, sems.at[n])
        for n, (source, target) in enumerate(((k_in, k), (v_in, v), (q_in, q), (g_in, g)))
    ]
    for copy in copies:
        copy.start()
    copies[0].wait()
    copies[1].wait()
    fan = kv_out.shape[0] // HEADS
    for j in range(HEADS):
        both = jnp.concatenate([k[:, j * D : (j + 1) * D], v[:, j * D : (j + 1) * D]], axis=1)
        for f in range(fan):
            kv_out[j * fan + f] = both
    h = head[0]
    copies[2].wait()
    copies[3].wait()
    for x in range(HEADS):
        cols = pl.ds(mo((h ^ x) * (G * D), G * D), G * D)
        sends[x][:, : G * D] = q[:, cols]
        sends[x][:, G * D :] = g[:, cols]


def collect_body(*refs):
    parts, (queries, grads) = refs[:HEADS], refs[HEADS:]
    for x in range(HEADS):
        queries[x] = parts[x][:, : G * D]
        grads[x] = parts[x][:, G * D :]


def tiles_needed(meta, nq, nk, t, kb):
    last = meta[nq + nk + t * TB + TB - 1]
    need = jnp.int32(0)
    for j in range(nk // kb):
        need += (meta[2 * nq + nk + j * kb] <= last).astype(jnp.int32)
    return need


def in_pairs(need, step, width, state):
    state = lax.fori_loop(0, need // 2, functools.partial(step, 2 * width), state)
    return lax.fori_loop(need // 2 * 2, need, functools.partial(step, width), state)


def query_lane(meta, nq, nk, t):
    lane = lax.broadcasted_iota(jnp.int32, (1, ROWS), 1)
    block = (lane // BLK) % TB
    pos = jnp.zeros((1, ROWS), jnp.int32)
    for b in range(TB):
        pos = jnp.where(block == b, meta[nq + nk + t * TB + b], pos)
    return pos * BLK + lane % BLK


def masked_scores(meta, nq, nk, scores, lane_pos, first):
    row = lax.broadcasted_iota(jnp.int32, (BLK, ROWS), 0)
    parts = []
    for b in range(scores.shape[0] // BLK):
        at = meta[2 * nq + nk + first + b] * BLK
        allowed = row <= lane_pos - at
        parts.append(jnp.where(allowed, scores[b * BLK : (b + 1) * BLK], LOW))
    return jnp.concatenate(parts, axis=0)


def dot(a, b):
    return lax.dot_general(a, b, (((1,), (0,)), ((), ())), preferred_element_type=F32)


def row_slots(meta, cn):
    for r in range(cn):
        for x in range(HEADS):
            n = meta[r * HEADS + x]
            yield r, x, (n // TB) * ROWS + (n % TB) * BLK


def rows_at(base, g):
    return pl.ds(mo(base + g * TB * BLK, BLK), BLK)


def stage_body(cn, meta, *refs):
    parts, (rows, tiles) = refs[:cn], refs[cn:]
    for r, x, base in row_slots(meta, cn):
        for g in range(G):
            rows[rows_at(base, g), :] = parts[r][x, :, g * D : (g + 1) * D]
    for t in range(tiles.shape[0]):
        tiles[t] = rows[t * ROWS : (t + 1) * ROWS, :].T


def stage_keys_body(nq, nk, meta, kv_near, kv_far, ks, vs, vt):
    for s in range(nk):
        at = pl.ds(mo(meta[nq + s] * BLK, BLK), BLK)
        kv = (kv_near, kv_far)[s // (nk // 2)]
        ks[at, :] = kv[s % (nk // 2), :, :D]
        vs[at, :] = kv[s % (nk // 2), :, D:]
    for j in range(vt.shape[0]):
        vt[j] = vs[j * TK : (j + 1) * TK, :].T


def forward_body(nq, nk, meta, qt, ks, vt, logs, ot, weights_out, sbuf):
    def tile(t, unused):
        need = tiles_needed(meta, nq, nk, t, KB)
        lane_pos = query_lane(meta, nq, nk, t)
        query = qt[t]

        def score(width, j, run):
            for c in range(0, width, SUB):
                at = pl.ds(mo(j * width + c, SUB), SUB)
                scores = dot(ks[at, :], query)
                scores = masked_scores(meta, nq, nk, scores, lane_pos, (j * width + c) // BLK)
                sbuf[at, :] = scores
                run = jnp.maximum(run, jnp.max(scores, axis=0, keepdims=True))
            return run

        top = in_pairs(need, score, TK, jnp.full((1, ROWS), LOW * 0.1, F32)) * C2

        def step(width, j, state):
            total, acc = state
            for c in range(0, width, SUB):
                at = pl.ds(mo(j * width + c, SUB), SUB)
                weights = jnp.exp2(sbuf[at, :] * C2 - top)
                total += jnp.sum(weights, axis=0, keepdims=True)
                rounded = weights.astype(BF)
                weights_out[t, at, :] = rounded
                acc += dot(vt[j * (width // TK) + c // TK, :, c % TK : c % TK + SUB], rounded)
            return total, acc

        state = (jnp.zeros((1, ROWS), F32), jnp.zeros((D, ROWS), F32))
        total, acc = in_pairs(need, step, TK, state)
        some = total > 0.0
        safe = jnp.where(some, total, 1.0)
        lanes = pl.ds(mo(t * ROWS, ROWS), ROWS)
        logs[0:1, lanes] = jnp.where(some, top + jnp.log2(safe), LOW)
        logs[1:2, lanes] = top
        ot[t] = acc * jnp.where(some, 1.0 / safe, 0.0)
        return unused

    lax.fori_loop(0, nq // TB, tile, 0)


def delta_body(cn, meta, logs, ot, *refs):
    parts, (stats, gt, gn) = refs[:cn], refs[cn:]
    for r, x, base in row_slots(meta, cn):
        for g in range(G):
            gn[rows_at(base, g), :] = parts[r][x, :, g * D : (g + 1) * D]
    stats[0:1, :] = logs[0:1, :]
    for t in range(gt.shape[0]):
        lanes = slice(t * ROWS, (t + 1) * ROWS)
        grads = gn[lanes, :].T
        gt[t] = grads
        stats[1:2, lanes] = jnp.sum(ot[t] * grads.astype(F32), axis=0, keepdims=True)


def attended_body(cn, meta, ot, ks, *refs):
    outs, kt, on = refs[:cn], refs[cn], refs[cn + 1]
    for t in range(ot.shape[0]):
        on[t * ROWS : (t + 1) * ROWS, :] = ot[t].astype(BF).T
    for r, x, base in row_slots(meta, cn):
        for g in range(G):
            outs[r][x, :, g * D : (g + 1) * D] = on[rows_at(base, g), :]
    for j in range(kt.shape[0]):
        kt[j] = ks[j * TK : (j + 1) * TK, :].T


def combine(stats):
    logs = [s[0:1, :] for s in stats]
    top = functools.reduce(jnp.maximum, logs)
    parts = [jnp.exp2(log - top) for log in logs]
    whole = functools.reduce(jnp.add, parts)
    return parts, whole, top


def backward_body(cn, nk, meta, *refs):
    stats = refs[:cn]
    logs, qn, gt, kt, vs, weights = refs[cn : cn + 6]
    near, far, *outs = refs[cn + 6 : 2 * cn + 8]
    dk, dv, dqt, dqn, gn, scale_all, delta_all = refs[2 * cn + 8 :]
    nq = cn * HEADS
    nt = nq // TB

    parts, whole, top = combine(stats)
    scale_all[...] = jnp.exp2(logs[1:2, :] - top) / whole
    delta_all[...] = functools.reduce(jnp.add, [p * s[1:2, :] for p, s in zip(parts, stats)]) / whole
    dk[...] = jnp.zeros_like(dk)
    dv[...] = jnp.zeros_like(dv)

    def tile(t, unused):
        need = tiles_needed(meta, nq, nk, t, SUB // BLK)
        lanes = pl.ds(mo(t * ROWS, ROWS), ROWS)
        scale, delta = scale_all[:, lanes], delta_all[:, lanes]
        gn[...] = (gt[t].astype(F32) * scale).astype(BF).T
        dqt[...] = jnp.zeros_like(dqt)

        def step(width, j, state):
            for c in range(0, width, SUB):
                keys = pl.ds(mo(j * width + c, SUB), SUB)
                own = weights[t, keys, :]
                lean = (dot(vs[keys, :], gt[t]) - delta) * scale
                grad_scores = (own.astype(F32) * lean).astype(BF)
                dv[keys, :] += dot(own, gn[...])
                dk[keys, :] += dot(grad_scores, qn[lanes, :])
                dqt[...] += dot(kt[j * width // TK, :, c : c + SUB], grad_scores)
            return state

        in_pairs(need, step, SUB, 0)
        dqn[lanes, :] = (dqt[...] * SCALE).astype(BF).T
        return unused

    lax.fori_loop(0, nt, tile, 0)
    for s in range(nk):
        at = pl.ds(mo(meta[nq + s] * BLK, BLK), BLK)
        kv_out = (near, far)[s // (nk // 2)]
        kv_out[s % (nk // 2), :, :D] = (dk[at, :] * SCALE).astype(BF)
        kv_out[s % (nk // 2), :, D:] = dv[at, :].astype(BF)
    for r, x, base in row_slots(meta, cn):
        for g in range(G):
            outs[r][x, :, g * D : (g + 1) * D] = dqn[rows_at(base, g), :]


def add_body(one, two, out):
    out[...] = (one[...].astype(F32) + two[...].astype(F32)).astype(BF)


def sum_body(cn, meta, *refs):
    stats, attended, grads = refs[:cn], refs[cn : 2 * cn], refs[2 * cn : 3 * cn]
    outs, columns = refs[3 * cn : 3 * cn + HEADS], refs[3 * cn + HEADS]
    parts, whole, top = combine(stats)
    inverse = 1.0 / whole
    spread = D // cn
    tall = jnp.concatenate([jnp.broadcast_to(p * inverse, (spread, p.shape[1])) for p in parts], axis=0)
    for t in range(tall.shape[1] // ROWS):
        columns[t * ROWS : (t + 1) * ROWS, :] = tall[:, t * ROWS : (t + 1) * ROWS].T
    for r, x, base in row_slots(meta, 1):
        for g in range(G):
            cols = slice(g * D, (g + 1) * D)
            column = columns[rows_at(base, g), :]
            total = jnp.zeros((BLK, D), F32)
            for i in range(cn):
                total += column[:, i * spread : i * spread + 1] * attended[i][x, :, cols].astype(F32)
            outs[x][:, cols] = total.astype(BF)
        total = grads[0][x].astype(F32)
        for i in range(1, cn):
            total += grads[i][x].astype(F32)
        outs[x][:, G * D :] = total.astype(BF)


def place_body(head, *refs):
    parts, shares = refs[:HEADS], refs[HEADS]
    attended, grad, dk, dv = refs[HEADS + 1 :]
    h = head[0]
    for x in range(HEADS):
        cols = pl.ds(mo((h ^ x) * (G * D), G * D), G * D)
        attended[:, cols] = parts[x][:, : G * D]
        grad[:, cols] = parts[x][:, G * D :]
    fan = shares.shape[0] // HEADS
    for j in range(HEADS):
        total = shares[j * fan].astype(F32)
        for f in range(1, fan):
            total += shares[j * fan + f].astype(F32)
        dk[:, j * D : (j + 1) * D] = total[:, :D].astype(BF)
        dv[:, j * D : (j + 1) * D] = total[:, D:].astype(BF)


def flip(axis, value, x):
    return lax.ppermute(value, axis, [(j, j ^ x) for j in range(HEADS)])


def per_device(queries, keys, values, grad_out, block_order):
    xs, zs, ys = lax.axis_size("xlo"), lax.axis_size("z"), lax.axis_size("inner")
    head, core = lax.axis_index(XAXES), lax.axis_index("core")
    z, inner = lax.axis_index("z"), lax.axis_index("inner")
    shifts = range(ys)
    cn = ys
    nq = cn * HEADS
    n = HEADS * zs
    nk = 2 * n

    def share(value, shift, back=False):
        step = ys - shift if back else shift
        return lax.ppermute(value, "inner", [(j, (j + step) % ys) for j in range(ys)])

    def cross(value):
        return lax.ppermute(value, "core", [(0, 1), (1, 0)])

    def block_of(x, c, j, k):
        return (((x // xs * 2 + c) * xs + x % xs) * zs + j) * ys + k

    slot = jnp.arange(nq, dtype=jnp.int32)
    q_block = block_of(head ^ (slot % HEADS), core, z, (inner - slot // HEADS) % ys)
    slot = jnp.arange(nk, dtype=jnp.int32)
    k_block = block_of((slot % n) // zs, core ^ (slot // n), slot % zs, inner)
    every = jnp.arange(block_order.shape[0], dtype=jnp.int32)

    def ranked(block):
        pos = jnp.sum(jnp.where(block[:, None] == every[None, :], block_order[None, :], 0), axis=1)
        rank = jnp.sum((pos[None, :] < pos[:, None]).astype(jnp.int32), axis=1)
        n = block.shape[0]
        hit = rank[None, :] == jnp.arange(n, dtype=jnp.int32)[:, None]
        return rank, jnp.sum(jnp.where(hit, pos[None, :], 0), axis=1)

    q_rank, q_sorted = ranked(q_block)
    k_rank, k_sorted = ranked(k_block)
    meta = jnp.concatenate([q_rank, k_rank, q_sorted, k_sorted])
    head_word = head[None].astype(jnp.int32)

    wide, quad = sds((BLK, 2 * G * D), BF), sds((HEADS, BLK, G * D), BF)
    full_in, thin_in = pltpu.VMEM(queries.shape, BF), pltpu.VMEM(keys.shape, BF)
    *sends, kv_send = call(
        pack_body,
        (wide,) * HEADS + (sds((n, BLK, 2 * D), BF),),
        1,
        4,
        [full_in, thin_in, thin_in, full_in, pltpu.SemaphoreType.DMA((4,))],
        space=HBM,
        limit=60 * 1024 * 1024,
    )(head_word, queries, keys, values, grad_out)
    with jax.named_scope("keys_in"):
        kv = lax.all_to_all(kv_send, XAXES + ("z",), split_axis=0, concat_axis=0, tiled=True)

    def spread(mine):
        return [mine] + [share(mine, shift) for shift in shifts[1:]]

    nrow, nkey = nq * BLK * G, nk * BLK
    nt, nj = nq // TB, nk // KB
    tiles = sds((nt, D, ROWS), BF)
    rows = sds((nrow, D), BF)
    key_rows = sds((nkey, D), BF)
    pairs = sds((nt, nkey, ROWS), BF)
    stat = sds((2, nrow), F32)
    work = nrow * nkey
    with jax.named_scope("queries_in"):
        arrived = [sends[0]] + [flip(XAXES, sends[x], x) for x in range(1, HEADS)]
        arrived, meta = lax.optimization_barrier((arrived, meta))
        q_mine, g_mine = call(collect_body, (quad, quad), 0, HEADS)(*arrived)
        q_all = spread(q_mine)
    with jax.named_scope("keys_cross_in"):
        q_all, g_mine, kv = lax.optimization_barrier((q_all, g_mine, kv))
        ks, vs, vt = call(
            functools.partial(stage_keys_body, nq, nk), (key_rows, key_rows, sds((nj, D, TK), BF)), 1, 2
        )(meta, kv, cross(kv))
    with jax.named_scope("queries_in"):
        qn, qt = call(functools.partial(stage_body, cn), (rows, tiles), 1, cn)(meta, *q_all)
    with jax.named_scope("grads_in"):
        g_all = spread(g_mine)
    logs, ot, weights = call(
        functools.partial(forward_body, nq, nk),
        (stat, sds((nt, D, ROWS), F32), pairs),
        1,
        3,
        [pltpu.VMEM((nkey, ROWS), F32)],
        pl.CostEstimate(flops=4 * work * D, bytes_accessed=1 << 22, transcendentals=work),
    )(meta, qt, ks, vt)
    stats, gt = call(
        functools.partial(delta_body, cn), (stat, tiles), 1, cn + 2, [pltpu.VMEM((nrow, D), BF)]
    )(meta, logs, ot, *g_all)
    with jax.named_scope("stats"):
        all_stats = [stats] + [share(stats, shift) for shift in shifts[1:]]
    with jax.named_scope("attended_out"):
        late_ot, _ = lax.optimization_barrier((ot, stats))
        *o_parts, kt = call(
            functools.partial(attended_body, cn),
            (quad,) * cn + (sds((nj, D, TK), BF),),
            1,
            2,
            [pltpu.VMEM((nrow, D), BF)],
            pl.CostEstimate(flops=0, bytes_accessed=1 << 22, transcendentals=0),
        )(meta, late_ot, ks)
        o_back = [o_parts[0]] + [share(part, shift, True) for part, shift in zip(o_parts[1:], shifts[1:])]
    kv_near, kv_far, *q_parts = call(
        functools.partial(backward_body, cn, nk),
        (sds((n, BLK, 2 * D), BF),) * 2 + (quad,) * cn,
        1,
        cn + 6,
        [
            pltpu.VMEM((nkey, D), F32),
            pltpu.VMEM((nkey, D), F32),
            pltpu.VMEM((D, ROWS), F32),
            pltpu.VMEM((nrow, D), BF),
            pltpu.VMEM((ROWS, D), BF),
            pltpu.VMEM((1, nrow), F32),
            pltpu.VMEM((1, nrow), F32),
        ],
        pl.CostEstimate(flops=8 * work * D, bytes_accessed=1 << 22, transcendentals=0),
    )(meta, *all_stats, logs, qn, gt, kt, vs, weights)
    with jax.named_scope("keys_out"):
        kv_near, kv_far, q_parts, o_back = lax.optimization_barrier((kv_near, kv_far, q_parts, o_back))
        kv_part = call(add_body, sds((n, BLK, 2 * D), BF), 0, 2)(kv_near, cross(kv_far))
        kv_parts = lax.all_to_all(kv_part, XAXES + ("z",), split_axis=0, concat_axis=0, tiled=True)
    opposite = [(ys - shift) % ys for shift in shifts]
    with jax.named_scope("queries_out"):
        back = [q_parts[0]] + [share(part, shift, True) for part, shift in zip(q_parts[1:], shifts[1:])]
        sums = call(
            functools.partial(sum_body, cn), (wide,) * HEADS, 1, 3 * cn, [pltpu.VMEM((nrow, D), F32)]
        )(meta, *[all_stats[i] for i in opposite], *o_back, *back)
        final = [sums[0]] + [flip(XAXES, sums[x], x) for x in range(1, HEADS)]
    full, thin = sds(queries.shape, BF), sds(keys.shape, BF)
    return call(place_body, (full, full, thin, thin), 1, HEADS + 1)(head_word, *final, kv_parts)


def solution(mesh):
    heads, outer, inner = (mesh.shape[name] for name in ("head", "outer", "inner"))
    names = ("xhi", "core", "xlo", "z", "inner")
    split = Mesh(mesh.devices.reshape(heads // 2, 2, 2, outer // 2, inner), names)
    rows = P(names, None)
    return jax.shard_map(
        per_device,
        mesh=split,
        in_specs=(rows, rows, rows, rows, P()),
        out_specs=(rows, rows, rows, rows),
        check_vma=False,
    )
```

```python
import functools
import math

import jax
import jax.numpy as jnp
from jax import lax
from jax.experimental import pallas as pl
from jax.experimental.pallas import tpu as pltpu
from jax.sharding import Mesh, PartitionSpec as P

D = 128
BLK = 32
G = 4
HEADS = 4
TB = 4
ROWS = TB * BLK * G
KB = 16
TK = KB * BLK
SUB = 256
SCALE = 1.0 / math.sqrt(D)
C2 = SCALE * math.log2(math.e)
LOW = -1e30
XAXES = ("xhi", "xlo")
LIMIT = 20 * 1024 * 1024
F32, BF = jnp.float32, jnp.bfloat16
VMEM = pl.BlockSpec(memory_space=pltpu.VMEM)
HBM = pl.BlockSpec(memory_space=pltpu.HBM)
SMEM = pl.BlockSpec(memory_space=pltpu.SMEM)


def mo(value, by):
    return pl.multiple_of(value, by)


def call(body, out_shape, n_smem, n_in, scratch=(), cost=None, space=VMEM, limit=LIMIT):
    return pl.pallas_call(
        body,
        out_shape=out_shape,
        in_specs=[SMEM] * n_smem + [space] * n_in,
        out_specs=jax.tree.map(lambda _: VMEM, out_shape),
        scratch_shapes=list(scratch),
        compiler_params=pltpu.CompilerParams(vmem_limit_bytes=limit),
        cost_estimate=cost,
    )


def sds(shape, dtype):
    return jax.ShapeDtypeStruct(shape, dtype)


def pack_body(head, q_in, k_in, v_in, g_in, *refs):
    sends, kv_out = refs[:HEADS], refs[HEADS]
    q, k, v, g, sems = refs[HEADS + 1 :]
    copies = [
        pltpu.make_async_copy(source, target, sems.at[n])
        for n, (source, target) in enumerate(((k_in, k), (v_in, v), (q_in, q), (g_in, g)))
    ]
    for copy in copies:
        copy.start()
    copies[0].wait()
    copies[1].wait()
    fan = kv_out.shape[0] // HEADS
    for j in range(HEADS):
        both = jnp.concatenate([k[:, j * D : (j + 1) * D], v[:, j * D : (j + 1) * D]], axis=1)
        for f in range(fan):
            kv_out[j * fan + f] = both
    h = head[0]
    copies[2].wait()
    copies[3].wait()
    for x in range(HEADS):
        cols = pl.ds(mo((h ^ x) * (G * D), G * D), G * D)
        sends[x][:, : G * D] = q[:, cols]
        sends[x][:, G * D :] = g[:, cols]


def collect_body(*refs):
    parts, (queries, grads) = refs[:HEADS], refs[HEADS:]
    for x in range(HEADS):
        queries[x] = parts[x][:, : G * D]
        grads[x] = parts[x][:, G * D :]


def tiles_needed(meta, nq, nk, t, kb):
    last = meta[nq + nk + t * TB + TB - 1]
    need = jnp.int32(0)
    for j in range(nk // kb):
        need += (meta[2 * nq + nk + j * kb] <= last).astype(jnp.int32)
    return need


def in_pairs(need, step, width, state):
    state = lax.fori_loop(0, need // 2, functools.partial(step, 2 * width), state)
    return lax.fori_loop(need // 2 * 2, need, functools.partial(step, width), state)


def query_lane(meta, nq, nk, t):
    lane = lax.broadcasted_iota(jnp.int32, (1, ROWS), 1)
    block = (lane // BLK) % TB
    pos = jnp.zeros((1, ROWS), jnp.int32)
    for b in range(TB):
        pos = jnp.where(block == b, meta[nq + nk + t * TB + b], pos)
    return pos * BLK + lane % BLK


def masked_scores(meta, nq, nk, scores, lane_pos, first):
    row = lax.broadcasted_iota(jnp.int32, (BLK, ROWS), 0)
    parts = []
    for b in range(scores.shape[0] // BLK):
        at = meta[2 * nq + nk + first + b] * BLK
        allowed = row <= lane_pos - at
        parts.append(jnp.where(allowed, scores[b * BLK : (b + 1) * BLK], LOW))
    return jnp.concatenate(parts, axis=0)


def dot(a, b):
    return lax.dot_general(a, b, (((1,), (0,)), ((), ())), preferred_element_type=F32)


def row_slots(meta, cn):
    for r in range(cn):
        for x in range(HEADS):
            n = meta[r * HEADS + x]
            yield r, x, (n // TB) * ROWS + (n % TB) * BLK


def rows_at(base, g):
    return pl.ds(mo(base + g * TB * BLK, BLK), BLK)


def stage_body(cn, meta, *refs):
    parts, (rows, tiles) = refs[:cn], refs[cn:]
    for r, x, base in row_slots(meta, cn):
        for g in range(G):
            rows[rows_at(base, g), :] = parts[r][x, :, g * D : (g + 1) * D]
    for t in range(tiles.shape[0]):
        tiles[t] = rows[t * ROWS : (t + 1) * ROWS, :].T


def stage_keys_body(nq, nk, meta, kv_near, kv_far, ks, vs, vt):
    for s in range(nk):
        at = pl.ds(mo(meta[nq + s] * BLK, BLK), BLK)
        kv = (kv_near, kv_far)[s // (nk // 2)]
        ks[at, :] = kv[s % (nk // 2), :, :D]
        vs[at, :] = kv[s % (nk // 2), :, D:]
    for j in range(vt.shape[0]):
        vt[j] = vs[j * TK : (j + 1) * TK, :].T


def forward_body(nq, nk, meta, qt, ks, vt, logs, ot, weights_out, sbuf):
    def tile(t, unused):
        need = tiles_needed(meta, nq, nk, t, KB)
        lane_pos = query_lane(meta, nq, nk, t)
        query = qt[t]

        def score(width, j, run):
            for c in range(0, width, SUB):
                at = pl.ds(mo(j * width + c, SUB), SUB)
                scores = dot(ks[at, :], query)
                scores = masked_scores(meta, nq, nk, scores, lane_pos, (j * width + c) // BLK)
                sbuf[at, :] = scores
                run = jnp.maximum(run, jnp.max(scores, axis=0, keepdims=True))
            return run

        top = in_pairs(need, score, TK, jnp.full((1, ROWS), LOW * 0.1, F32)) * C2

        def step(width, j, state):
            total, acc = state
            for c in range(0, width, SUB):
                at = pl.ds(mo(j * width + c, SUB), SUB)
                weights = jnp.exp2(sbuf[at, :] * C2 - top)
                total += jnp.sum(weights, axis=0, keepdims=True)
                rounded = weights.astype(BF)
                weights_out[t, at, :] = rounded
                acc += dot(vt[j * (width // TK) + c // TK, :, c % TK : c % TK + SUB], rounded)
            return total, acc

        state = (jnp.zeros((1, ROWS), F32), jnp.zeros((D, ROWS), F32))
        total, acc = in_pairs(need, step, TK, state)
        some = total > 0.0
        safe = jnp.where(some, total, 1.0)
        lanes = pl.ds(mo(t * ROWS, ROWS), ROWS)
        logs[0:1, lanes] = jnp.where(some, top + jnp.log2(safe), LOW)
        logs[1:2, lanes] = top
        ot[t] = acc * jnp.where(some, 1.0 / safe, 0.0)
        return unused

    lax.fori_loop(0, nq // TB, tile, 0)


def delta_body(cn, meta, logs, ot, *refs):
    parts, (stats, gt, gn) = refs[:cn], refs[cn:]
    for r, x, base in row_slots(meta, cn):
        for g in range(G):
            gn[rows_at(base, g), :] = parts[r][x, :, g * D : (g + 1) * D]
    stats[0:1, :] = logs[0:1, :]
    for t in range(gt.shape[0]):
        lanes = slice(t * ROWS, (t + 1) * ROWS)
        grads = gn[lanes, :].T
        gt[t] = grads
        stats[1:2, lanes] = jnp.sum(ot[t] * grads.astype(F32), axis=0, keepdims=True)


def attended_body(cn, meta, ot, ks, *refs):
    outs, kt, on = refs[:cn], refs[cn], refs[cn + 1]
    for t in range(ot.shape[0]):
        on[t * ROWS : (t + 1) * ROWS, :] = ot[t].astype(BF).T
    for r, x, base in row_slots(meta, cn):
        for g in range(G):
            outs[r][x, :, g * D : (g + 1) * D] = on[rows_at(base, g), :]
    for j in range(kt.shape[0]):
        kt[j] = ks[j * TK : (j + 1) * TK, :].T


def combine(stats):
    logs = [s[0:1, :] for s in stats]
    top = functools.reduce(jnp.maximum, logs)
    parts = [jnp.exp2(log - top) for log in logs]
    whole = functools.reduce(jnp.add, parts)
    return parts, whole, top


def backward_body(cn, nk, meta, *refs):
    stats = refs[:cn]
    logs, qn, gt, kt, vs, weights = refs[cn : cn + 6]
    near, far, *outs = refs[cn + 6 : 2 * cn + 8]
    dk, dv, dqt, dqn, gn, scale_all, delta_all = refs[2 * cn + 8 :]
    nq = cn * HEADS
    nt = nq // TB

    parts, whole, top = combine(stats)
    scale_all[...] = jnp.exp2(logs[1:2, :] - top) / whole
    delta_all[...] = functools.reduce(jnp.add, [p * s[1:2, :] for p, s in zip(parts, stats)]) / whole
    dk[...] = jnp.zeros_like(dk)
    dv[...] = jnp.zeros_like(dv)

    def tile(t, unused):
        need = tiles_needed(meta, nq, nk, t, SUB // BLK)
        lanes = pl.ds(mo(t * ROWS, ROWS), ROWS)
        scale, delta = scale_all[:, lanes], delta_all[:, lanes]
        gn[...] = (gt[t].astype(F32) * scale).astype(BF).T
        dqt[...] = jnp.zeros_like(dqt)

        def step(width, j, state):
            for c in range(0, width, SUB):
                keys = pl.ds(mo(j * width + c, SUB), SUB)
                own = weights[t, keys, :]
                lean = (dot(vs[keys, :], gt[t]) - delta) * scale
                grad_scores = (own.astype(F32) * lean).astype(BF)
                dv[keys, :] += dot(own, gn[...])
                dk[keys, :] += dot(grad_scores, qn[lanes, :])
                dqt[...] += dot(kt[j * width // TK, :, c : c + SUB], grad_scores)
            return state

        in_pairs(need, step, SUB, 0)
        dqn[lanes, :] = (dqt[...] * SCALE).astype(BF).T
        return unused

    lax.fori_loop(0, nt, tile, 0)
    for s in range(nk):
        at = pl.ds(mo(meta[nq + s] * BLK, BLK), BLK)
        kv_out = (near, far)[s // (nk // 2)]
        kv_out[s % (nk // 2), :, :D] = (dk[at, :] * SCALE).astype(BF)
        kv_out[s % (nk // 2), :, D:] = dv[at, :].astype(BF)
    for r, x, base in row_slots(meta, cn):
        for g in range(G):
            outs[r][x, :, g * D : (g + 1) * D] = dqn[rows_at(base, g), :]


def add_body(one, two, out):
    out[...] = (one[...].astype(F32) + two[...].astype(F32)).astype(BF)


def attended_sum_body(cn, meta, *refs):
    stats, attended, out, columns = refs[:cn], refs[cn : 2 * cn], refs[2 * cn], refs[2 * cn + 1]
    parts, whole, top = combine(stats)
    inverse = 1.0 / whole
    spread = D // cn
    tall = jnp.concatenate([jnp.broadcast_to(p * inverse, (spread, p.shape[1])) for p in parts], axis=0)
    for t in range(tall.shape[1] // ROWS):
        columns[t * ROWS : (t + 1) * ROWS, :] = tall[:, t * ROWS : (t + 1) * ROWS].T
    for r, x, base in row_slots(meta, 1):
        for g in range(G):
            cols = slice(g * D, (g + 1) * D)
            column = columns[rows_at(base, g), :]
            total = jnp.zeros((BLK, D), F32)
            for i in range(cn):
                total += column[:, i * spread : i * spread + 1] * attended[i][x, :, cols].astype(F32)
            out[x, :, cols] = total.astype(BF)


def sum_body(cn, attended, *refs):
    grads, outs = refs[:cn], refs[cn:]
    for x in range(HEADS):
        outs[x][:, : G * D] = attended[x]
        total = grads[0][x].astype(F32)
        for i in range(1, cn):
            total += grads[i][x].astype(F32)
        outs[x][:, G * D :] = total.astype(BF)


def place_body(head, *refs):
    parts, shares = refs[:HEADS], refs[HEADS]
    attended, grad, dk, dv = refs[HEADS + 1 :]
    h = head[0]
    for x in range(HEADS):
        cols = pl.ds(mo((h ^ x) * (G * D), G * D), G * D)
        attended[:, cols] = parts[x][:, : G * D]
        grad[:, cols] = parts[x][:, G * D :]
    fan = shares.shape[0] // HEADS
    for j in range(HEADS):
        total = shares[j * fan].astype(F32)
        for f in range(1, fan):
            total += shares[j * fan + f].astype(F32)
        dk[:, j * D : (j + 1) * D] = total[:, :D].astype(BF)
        dv[:, j * D : (j + 1) * D] = total[:, D:].astype(BF)


def flip(axis, value, x):
    return lax.ppermute(value, axis, [(j, j ^ x) for j in range(HEADS)])


def per_device(queries, keys, values, grad_out, block_order):
    xs, zs, ys = lax.axis_size("xlo"), lax.axis_size("z"), lax.axis_size("inner")
    head, core = lax.axis_index(XAXES), lax.axis_index("core")
    z, inner = lax.axis_index("z"), lax.axis_index("inner")
    shifts = range(ys)
    cn = ys
    nq = cn * HEADS
    n = HEADS * zs
    nk = 2 * n

    def share(value, shift, back=False):
        step = ys - shift if back else shift
        return lax.ppermute(value, "inner", [(j, (j + step) % ys) for j in range(ys)])

    def cross(value):
        return lax.ppermute(value, "core", [(0, 1), (1, 0)])

    def block_of(x, c, j, k):
        return (((x // xs * 2 + c) * xs + x % xs) * zs + j) * ys + k

    slot = jnp.arange(nq, dtype=jnp.int32)
    q_block = block_of(head ^ (slot % HEADS), core, z, (inner - slot // HEADS) % ys)
    slot = jnp.arange(nk, dtype=jnp.int32)
    k_block = block_of((slot % n) // zs, core ^ (slot // n), slot % zs, inner)
    every = jnp.arange(block_order.shape[0], dtype=jnp.int32)

    def ranked(block):
        pos = jnp.sum(jnp.where(block[:, None] == every[None, :], block_order[None, :], 0), axis=1)
        rank = jnp.sum((pos[None, :] < pos[:, None]).astype(jnp.int32), axis=1)
        n = block.shape[0]
        hit = rank[None, :] == jnp.arange(n, dtype=jnp.int32)[:, None]
        return rank, jnp.sum(jnp.where(hit, pos[None, :], 0), axis=1)

    q_rank, q_sorted = ranked(q_block)
    k_rank, k_sorted = ranked(k_block)
    meta = jnp.concatenate([q_rank, k_rank, q_sorted, k_sorted])
    head_word = head[None].astype(jnp.int32)

    wide, quad = sds((BLK, 2 * G * D), BF), sds((HEADS, BLK, G * D), BF)
    full_in, thin_in = pltpu.VMEM(queries.shape, BF), pltpu.VMEM(keys.shape, BF)
    *sends, kv_send = call(
        pack_body,
        (wide,) * HEADS + (sds((n, BLK, 2 * D), BF),),
        1,
        4,
        [full_in, thin_in, thin_in, full_in, pltpu.SemaphoreType.DMA((4,))],
        space=HBM,
        limit=60 * 1024 * 1024,
    )(head_word, queries, keys, values, grad_out)
    with jax.named_scope("keys_in"):
        kv = lax.all_to_all(kv_send, XAXES + ("z",), split_axis=0, concat_axis=0, tiled=True)

    def spread(mine):
        return [mine] + [share(mine, shift) for shift in shifts[1:]]

    nrow, nkey = nq * BLK * G, nk * BLK
    nt, nj = nq // TB, nk // KB
    tiles = sds((nt, D, ROWS), BF)
    rows = sds((nrow, D), BF)
    key_rows = sds((nkey, D), BF)
    pairs = sds((nt, nkey, ROWS), BF)
    stat = sds((2, nrow), F32)
    work = nrow * nkey
    with jax.named_scope("queries_in"):
        arrived = [sends[0]] + [flip(XAXES, sends[x], x) for x in range(1, HEADS)]
        arrived, meta = lax.optimization_barrier((arrived, meta))
        q_mine, g_mine = call(collect_body, (quad, quad), 0, HEADS)(*arrived)
        q_all = spread(q_mine)
    with jax.named_scope("keys_cross_in"):
        q_all, g_mine, kv = lax.optimization_barrier((q_all, g_mine, kv))
        ks, vs, vt = call(
            functools.partial(stage_keys_body, nq, nk), (key_rows, key_rows, sds((nj, D, TK), BF)), 1, 2
        )(meta, kv, cross(kv))
    with jax.named_scope("queries_in"):
        qn, qt = call(functools.partial(stage_body, cn), (rows, tiles), 1, cn)(meta, *q_all)
    with jax.named_scope("grads_in"):
        g_all = spread(g_mine)
    logs, ot, weights = call(
        functools.partial(forward_body, nq, nk),
        (stat, sds((nt, D, ROWS), F32), pairs),
        1,
        3,
        [pltpu.VMEM((nkey, ROWS), F32)],
        pl.CostEstimate(flops=4 * work * D, bytes_accessed=1 << 22, transcendentals=work),
    )(meta, qt, ks, vt)
    stats, gt = call(
        functools.partial(delta_body, cn), (stat, tiles), 1, cn + 2, [pltpu.VMEM((nrow, D), BF)]
    )(meta, logs, ot, *g_all)
    with jax.named_scope("stats"):
        all_stats = [stats] + [share(stats, shift) for shift in shifts[1:]]
    with jax.named_scope("attended_out"):
        late_ot, _ = lax.optimization_barrier((ot, stats))
        *o_parts, kt = call(
            functools.partial(attended_body, cn),
            (quad,) * cn + (sds((nj, D, TK), BF),),
            1,
            2,
            [pltpu.VMEM((nrow, D), BF)],
            pl.CostEstimate(flops=0, bytes_accessed=1 << 22, transcendentals=0),
        )(meta, late_ot, ks)
        o_back = [o_parts[0]] + [share(part, shift, True) for part, shift in zip(o_parts[1:], shifts[1:])]
    kv_near, kv_far, *q_parts = call(
        functools.partial(backward_body, cn, nk),
        (sds((n, BLK, 2 * D), BF),) * 2 + (quad,) * cn,
        1,
        cn + 6,
        [
            pltpu.VMEM((nkey, D), F32),
            pltpu.VMEM((nkey, D), F32),
            pltpu.VMEM((D, ROWS), F32),
            pltpu.VMEM((nrow, D), BF),
            pltpu.VMEM((ROWS, D), BF),
            pltpu.VMEM((1, nrow), F32),
            pltpu.VMEM((1, nrow), F32),
        ],
        pl.CostEstimate(flops=8 * work * D, bytes_accessed=1 << 22, transcendentals=0),
    )(meta, *all_stats, logs, qn, gt, kt, vs, weights)
    with jax.named_scope("keys_out"):
        kv_near, kv_far, q_parts, o_back = lax.optimization_barrier((kv_near, kv_far, q_parts, o_back))
        kv_part = call(add_body, sds((n, BLK, 2 * D), BF), 0, 2)(kv_near, cross(kv_far))
        kv_parts = lax.all_to_all(kv_part, XAXES + ("z",), split_axis=0, concat_axis=0, tiled=True)
    opposite = [(ys - shift) % ys for shift in shifts]
    with jax.named_scope("queries_out"):
        back = [q_parts[0]] + [share(part, shift, True) for part, shift in zip(q_parts[1:], shifts[1:])]
        late_stats = [all_stats[i] for i in opposite]
        kv_part, late_stats = lax.optimization_barrier((kv_part, late_stats))
        attended = call(
            functools.partial(attended_sum_body, cn),
            quad,
            1,
            2 * cn,
            [pltpu.VMEM((nrow, D), F32)],
            pl.CostEstimate(flops=0, bytes_accessed=1 << 22, transcendentals=0),
        )(meta, *late_stats, *o_back)
        sums = call(functools.partial(sum_body, cn), (wide,) * HEADS, 0, cn + 1)(attended, *back)
        final = [sums[0]] + [flip(XAXES, sums[x], x) for x in range(1, HEADS)]
    full, thin = sds(queries.shape, BF), sds(keys.shape, BF)
    return call(place_body, (full, full, thin, thin), 1, HEADS + 1)(head_word, *final, kv_parts)


def solution(mesh):
    heads, outer, inner = (mesh.shape[name] for name in ("head", "outer", "inner"))
    names = ("xhi", "core", "xlo", "z", "inner")
    split = Mesh(mesh.devices.reshape(heads // 2, 2, 2, outer // 2, inner), names)
    rows = P(names, None)
    return jax.shard_map(
        per_device,
        mesh=split,
        in_specs=(rows, rows, rows, rows, P()),
        out_specs=(rows, rows, rows, rows),
        check_vma=False,
    )
```

```python
import functools
import math

import jax
import jax.numpy as jnp
from jax import lax
from jax.experimental import pallas as pl
from jax.experimental.pallas import tpu as pltpu
from jax.sharding import Mesh, PartitionSpec as P

D = 128
BLK = 32
G = 4
HEADS = 4
TB = 4
ROWS = TB * BLK * G
KB = 16
TK = KB * BLK
SUB = 256
SCALE = 1.0 / math.sqrt(D)
C2 = SCALE * math.log2(math.e)
LOW = -1e30
XAXES = ("xhi", "xlo")
LIMIT = 20 * 1024 * 1024
F32, BF = jnp.float32, jnp.bfloat16
VMEM = pl.BlockSpec(memory_space=pltpu.VMEM)
HBM = pl.BlockSpec(memory_space=pltpu.HBM)
SMEM = pl.BlockSpec(memory_space=pltpu.SMEM)


def mo(value, by):
    return pl.multiple_of(value, by)


def call(body, out_shape, n_smem, n_in, scratch=(), cost=None, space=VMEM, limit=LIMIT):
    return pl.pallas_call(
        body,
        out_shape=out_shape,
        in_specs=[SMEM] * n_smem + [space] * n_in,
        out_specs=jax.tree.map(lambda _: VMEM, out_shape),
        scratch_shapes=list(scratch),
        compiler_params=pltpu.CompilerParams(vmem_limit_bytes=limit),
        cost_estimate=cost,
    )


def sds(shape, dtype):
    return jax.ShapeDtypeStruct(shape, dtype)


def pack_body(head, q_in, k_in, v_in, g_in, *refs):
    sends, kv_out = refs[:HEADS], refs[HEADS]
    q, k, v, g, sems = refs[HEADS + 1 :]
    copies = [
        pltpu.make_async_copy(source, target, sems.at[n])
        for n, (source, target) in enumerate(((k_in, k), (v_in, v), (q_in, q), (g_in, g)))
    ]
    for copy in copies:
        copy.start()
    copies[0].wait()
    copies[1].wait()
    fan = kv_out.shape[0] // HEADS
    for j in range(HEADS):
        both = jnp.concatenate([k[:, j * D : (j + 1) * D], v[:, j * D : (j + 1) * D]], axis=1)
        for f in range(fan):
            kv_out[j * fan + f] = both
    h = head[0]
    copies[2].wait()
    copies[3].wait()
    for x in range(HEADS):
        cols = pl.ds(mo((h ^ x) * (G * D), G * D), G * D)
        sends[x][:, : G * D] = q[:, cols]
        sends[x][:, G * D :] = g[:, cols]


def hold_body(rows, out):
    out[...] = rows[...]


def collect_body(*refs):
    parts, (queries, grads) = refs[:HEADS], refs[HEADS:]
    for x in range(HEADS):
        queries[x] = parts[x][:, : G * D]
        grads[x] = parts[x][:, G * D :]


def tiles_needed(meta, nq, nk, t, kb):
    last = meta[nq + nk + t * TB + TB - 1]
    need = jnp.int32(0)
    for j in range(nk // kb):
        need += (meta[2 * nq + nk + j * kb] <= last).astype(jnp.int32)
    return need


def in_pairs(need, step, width, state):
    state = lax.fori_loop(0, need // 2, functools.partial(step, 2 * width), state)
    return lax.fori_loop(need // 2 * 2, need, functools.partial(step, width), state)


def query_lane(meta, nq, nk, t):
    lane = lax.broadcasted_iota(jnp.int32, (1, ROWS), 1)
    block = (lane // BLK) % TB
    pos = jnp.zeros((1, ROWS), jnp.int32)
    for b in range(TB):
        pos = jnp.where(block == b, meta[nq + nk + t * TB + b], pos)
    return pos * BLK + lane % BLK


def masked_scores(meta, nq, nk, scores, lane_pos, first):
    row = lax.broadcasted_iota(jnp.int32, (BLK, ROWS), 0)
    parts = []
    for b in range(scores.shape[0] // BLK):
        at = meta[2 * nq + nk + first + b] * BLK
        allowed = row <= lane_pos - at
        parts.append(jnp.where(allowed, scores[b * BLK : (b + 1) * BLK], LOW))
    return jnp.concatenate(parts, axis=0)


def dot(a, b):
    return lax.dot_general(a, b, (((1,), (0,)), ((), ())), preferred_element_type=F32)


def row_slots(meta, cn):
    for r in range(cn):
        for x in range(HEADS):
            n = meta[r * HEADS + x]
            yield r, x, (n // TB) * ROWS + (n % TB) * BLK


def rows_at(base, g):
    return pl.ds(mo(base + g * TB * BLK, BLK), BLK)


def stage_body(cn, meta, *refs):
    parts, (rows, tiles) = refs[:cn], refs[cn:]
    for r, x, base in row_slots(meta, cn):
        for g in range(G):
            rows[rows_at(base, g), :] = parts[r][x, :, g * D : (g + 1) * D]
    for t in range(tiles.shape[0]):
        tiles[t] = rows[t * ROWS : (t + 1) * ROWS, :].T


def stage_keys_body(nq, nk, meta, kv_near, kv_far, ks, vs, vt):
    for s in range(nk):
        at = pl.ds(mo(meta[nq + s] * BLK, BLK), BLK)
        kv = (kv_near, kv_far)[s // (nk // 2)]
        ks[at, :] = kv[s % (nk // 2), :, :D]
        vs[at, :] = kv[s % (nk // 2), :, D:]
    for j in range(vt.shape[0]):
        vt[j] = vs[j * TK : (j + 1) * TK, :].T


def forward_body(nq, nk, meta, qt, ks, vt, logs, ot, weights_out, sbuf):
    def tile(t, unused):
        need = tiles_needed(meta, nq, nk, t, KB)
        lane_pos = query_lane(meta, nq, nk, t)
        query = qt[t]

        def score(width, j, run):
            for c in range(0, width, SUB):
                at = pl.ds(mo(j * width + c, SUB), SUB)
                scores = dot(ks[at, :], query)
                scores = masked_scores(meta, nq, nk, scores, lane_pos, (j * width + c) // BLK)
                sbuf[at, :] = scores
                run = jnp.maximum(run, jnp.max(scores, axis=0, keepdims=True))
            return run

        top = in_pairs(need, score, TK, jnp.full((1, ROWS), LOW * 0.1, F32)) * C2

        def step(width, j, state):
            total, acc = state
            for c in range(0, width, SUB):
                at = pl.ds(mo(j * width + c, SUB), SUB)
                weights = jnp.exp2(sbuf[at, :] * C2 - top)
                total += jnp.sum(weights, axis=0, keepdims=True)
                rounded = weights.astype(BF)
                weights_out[t, at, :] = rounded
                acc += dot(vt[j * (width // TK) + c // TK, :, c % TK : c % TK + SUB], rounded)
            return total, acc

        state = (jnp.zeros((1, ROWS), F32), jnp.zeros((D, ROWS), F32))
        total, acc = in_pairs(need, step, TK, state)
        some = total > 0.0
        safe = jnp.where(some, total, 1.0)
        lanes = pl.ds(mo(t * ROWS, ROWS), ROWS)
        logs[0:1, lanes] = jnp.where(some, top + jnp.log2(safe), LOW)
        logs[1:2, lanes] = top
        ot[t] = acc * jnp.where(some, 1.0 / safe, 0.0)
        return unused

    lax.fori_loop(0, nq // TB, tile, 0)


def delta_body(cn, meta, logs, ot, *refs):
    parts, (stats, gt, gn) = refs[:cn], refs[cn:]
    for r, x, base in row_slots(meta, cn):
        for g in range(G):
            gn[rows_at(base, g), :] = parts[r][x, :, g * D : (g + 1) * D]
    stats[0:1, :] = logs[0:1, :]
    for t in range(gt.shape[0]):
        lanes = slice(t * ROWS, (t + 1) * ROWS)
        grads = gn[lanes, :].T
        gt[t] = grads
        stats[1:2, lanes] = jnp.sum(ot[t] * grads.astype(F32), axis=0, keepdims=True)


def attended_body(cn, meta, ot, ks, *refs):
    outs, kt, on = refs[:cn], refs[cn], refs[cn + 1]
    for t in range(ot.shape[0]):
        on[t * ROWS : (t + 1) * ROWS, :] = ot[t].astype(BF).T
    for r, x, base in row_slots(meta, cn):
        for g in range(G):
            outs[r][x, :, g * D : (g + 1) * D] = on[rows_at(base, g), :]
    for j in range(kt.shape[0]):
        kt[j] = ks[j * TK : (j + 1) * TK, :].T


def combine(stats):
    logs = [s[0:1, :] for s in stats]
    top = functools.reduce(jnp.maximum, logs)
    parts = [jnp.exp2(log - top) for log in logs]
    whole = functools.reduce(jnp.add, parts)
    return parts, whole, top


def backward_body(cn, nk, meta, *refs):
    stats = refs[:cn]
    logs, qn, gt, kt, vs, weights = refs[cn : cn + 6]
    near, far, *outs = refs[cn + 6 : 2 * cn + 8]
    dk, dv, dqt, dqn, gn, scale_all, delta_all = refs[2 * cn + 8 :]
    nq = cn * HEADS
    nt = nq // TB

    parts, whole, top = combine(stats)
    scale_all[...] = jnp.exp2(logs[1:2, :] - top) / whole
    delta_all[...] = functools.reduce(jnp.add, [p * s[1:2, :] for p, s in zip(parts, stats)]) / whole
    dk[...] = jnp.zeros_like(dk)
    dv[...] = jnp.zeros_like(dv)

    def tile(t, unused):
        need = tiles_needed(meta, nq, nk, t, SUB // BLK)
        lanes = pl.ds(mo(t * ROWS, ROWS), ROWS)
        scale, delta = scale_all[:, lanes], delta_all[:, lanes]
        gn[...] = (gt[t].astype(F32) * scale).astype(BF).T
        dqt[...] = jnp.zeros_like(dqt)

        def step(width, j, state):
            for c in range(0, width, SUB):
                keys = pl.ds(mo(j * width + c, SUB), SUB)
                own = weights[t, keys, :]
                lean = (dot(vs[keys, :], gt[t]) - delta) * scale
                grad_scores = (own.astype(F32) * lean).astype(BF)
                dv[keys, :] += dot(own, gn[...])
                dk[keys, :] += dot(grad_scores, qn[lanes, :])
                dqt[...] += dot(kt[j * width // TK, :, c : c + SUB], grad_scores)
            return state

        in_pairs(need, step, SUB, 0)
        dqn[lanes, :] = (dqt[...] * SCALE).astype(BF).T
        return unused

    lax.fori_loop(0, nt, tile, 0)
    for s in range(nk):
        at = pl.ds(mo(meta[nq + s] * BLK, BLK), BLK)
        kv_out = (near, far)[s // (nk // 2)]
        kv_out[s % (nk // 2), :, :D] = (dk[at, :] * SCALE).astype(BF)
        kv_out[s % (nk // 2), :, D:] = dv[at, :].astype(BF)
    for r, x, base in row_slots(meta, cn):
        for g in range(G):
            outs[r][x, :, g * D : (g + 1) * D] = dqn[rows_at(base, g), :]


def add_body(one, two, out):
    out[...] = (one[...].astype(F32) + two[...].astype(F32)).astype(BF)


def attended_sum_body(cn, meta, *refs):
    stats, attended, out, columns = refs[:cn], refs[cn : 2 * cn], refs[2 * cn], refs[2 * cn + 1]
    parts, whole, top = combine(stats)
    inverse = 1.0 / whole
    spread = D // cn
    tall = jnp.concatenate([jnp.broadcast_to(p * inverse, (spread, p.shape[1])) for p in parts], axis=0)
    for t in range(tall.shape[1] // ROWS):
        columns[t * ROWS : (t + 1) * ROWS, :] = tall[:, t * ROWS : (t + 1) * ROWS].T
    for r, x, base in row_slots(meta, 1):
        for g in range(G):
            cols = slice(g * D, (g + 1) * D)
            column = columns[rows_at(base, g), :]
            total = jnp.zeros((BLK, D), F32)
            for i in range(cn):
                total += column[:, i * spread : i * spread + 1] * attended[i][x, :, cols].astype(F32)
            out[x, :, cols] = total.astype(BF)


def sum_body(cn, attended, *refs):
    grads, outs = refs[:cn], refs[cn:]
    for x in range(HEADS):
        outs[x][:, : G * D] = attended[x]
        total = grads[0][x].astype(F32)
        for i in range(1, cn):
            total += grads[i][x].astype(F32)
        outs[x][:, G * D :] = total.astype(BF)


def place_body(head, *refs):
    parts, shares = refs[:HEADS], refs[HEADS]
    attended, grad, dk, dv = refs[HEADS + 1 :]
    h = head[0]
    for x in range(HEADS):
        cols = pl.ds(mo((h ^ x) * (G * D), G * D), G * D)
        attended[:, cols] = parts[x][:, : G * D]
        grad[:, cols] = parts[x][:, G * D :]
    fan = shares.shape[0] // HEADS
    for j in range(HEADS):
        total = shares[j * fan].astype(F32)
        for f in range(1, fan):
            total += shares[j * fan + f].astype(F32)
        dk[:, j * D : (j + 1) * D] = total[:, :D].astype(BF)
        dv[:, j * D : (j + 1) * D] = total[:, D:].astype(BF)


def flip(axis, value, x):
    return lax.ppermute(value, axis, [(j, j ^ x) for j in range(HEADS)])


def per_device(queries, keys, values, grad_out, block_order):
    xs, zs, ys = lax.axis_size("xlo"), lax.axis_size("z"), lax.axis_size("inner")
    head, core = lax.axis_index(XAXES), lax.axis_index("core")
    z, inner = lax.axis_index("z"), lax.axis_index("inner")
    shifts = range(ys)
    cn = ys
    nq = cn * HEADS
    n = HEADS * zs
    nk = 2 * n

    def share(value, shift, back=False):
        step = ys - shift if back else shift
        return lax.ppermute(value, "inner", [(j, (j + step) % ys) for j in range(ys)])

    def cross(value):
        return lax.ppermute(value, "core", [(0, 1), (1, 0)])

    def block_of(x, c, j, k):
        return (((x // xs * 2 + c) * xs + x % xs) * zs + j) * ys + k

    slot = jnp.arange(nq, dtype=jnp.int32)
    q_block = block_of(head ^ (slot % HEADS), core, z, (inner - slot // HEADS) % ys)
    slot = jnp.arange(nk, dtype=jnp.int32)
    k_block = block_of((slot % n) // zs, core ^ (slot // n), slot % zs, inner)
    every = jnp.arange(block_order.shape[0], dtype=jnp.int32)

    def ranked(block):
        pos = jnp.sum(jnp.where(block[:, None] == every[None, :], block_order[None, :], 0), axis=1)
        rank = jnp.sum((pos[None, :] < pos[:, None]).astype(jnp.int32), axis=1)
        n = block.shape[0]
        hit = rank[None, :] == jnp.arange(n, dtype=jnp.int32)[:, None]
        return rank, jnp.sum(jnp.where(hit, pos[None, :], 0), axis=1)

    q_rank, q_sorted = ranked(q_block)
    k_rank, k_sorted = ranked(k_block)
    meta = jnp.concatenate([q_rank, k_rank, q_sorted, k_sorted])
    head_word = head[None].astype(jnp.int32)

    wide, quad = sds((BLK, 2 * G * D), BF), sds((HEADS, BLK, G * D), BF)
    full_in, thin_in = pltpu.VMEM(queries.shape, BF), pltpu.VMEM(keys.shape, BF)
    *sends, kv_send = call(
        pack_body,
        (wide,) * HEADS + (sds((n, BLK, 2 * D), BF),),
        1,
        4,
        [full_in, thin_in, thin_in, full_in, pltpu.SemaphoreType.DMA((4,))],
        space=HBM,
        limit=60 * 1024 * 1024,
    )(head_word, queries, keys, values, grad_out)
    with jax.named_scope("keys_in"):
        kv = lax.all_to_all(kv_send, XAXES + ("z",), split_axis=0, concat_axis=0, tiled=True)

    def spread(mine):
        return [mine] + [share(mine, shift) for shift in shifts[1:]]

    nrow, nkey = nq * BLK * G, nk * BLK
    nt, nj = nq // TB, nk // KB
    tiles = sds((nt, D, ROWS), BF)
    rows = sds((nrow, D), BF)
    key_rows = sds((nkey, D), BF)
    pairs = sds((nt, nkey, ROWS), BF)
    stat = sds((2, nrow), F32)
    work = nrow * nkey
    with jax.named_scope("queries_in"):
        held = call(hold_body, wide, 0, 1)(sends[0])
        arrived = [held] + [flip(XAXES, sends[x], x) for x in range(1, HEADS)]
        arrived, meta = lax.optimization_barrier((arrived, meta))
        q_mine, g_mine = call(collect_body, (quad, quad), 0, HEADS)(*arrived)
        q_all = spread(q_mine)
    with jax.named_scope("keys_cross_in"):
        q_all, g_mine, kv = lax.optimization_barrier((q_all, g_mine, kv))
        ks, vs, vt = call(
            functools.partial(stage_keys_body, nq, nk), (key_rows, key_rows, sds((nj, D, TK), BF)), 1, 2
        )(meta, kv, cross(kv))
    with jax.named_scope("queries_in"):
        qn, qt = call(functools.partial(stage_body, cn), (rows, tiles), 1, cn)(meta, *q_all)
    with jax.named_scope("grads_in"):
        g_all = spread(g_mine)
    logs, ot, weights = call(
        functools.partial(forward_body, nq, nk),
        (stat, sds((nt, D, ROWS), F32), pairs),
        1,
        3,
        [pltpu.VMEM((nkey, ROWS), F32)],
        pl.CostEstimate(flops=4 * work * D, bytes_accessed=1 << 22, transcendentals=work),
    )(meta, qt, ks, vt)
    stats, gt = call(
        functools.partial(delta_body, cn), (stat, tiles), 1, cn + 2, [pltpu.VMEM((nrow, D), BF)]
    )(meta, logs, ot, *g_all)
    with jax.named_scope("stats"):
        all_stats = [stats] + [share(stats, shift) for shift in shifts[1:]]
    with jax.named_scope("attended_out"):
        late_ot, _ = lax.optimization_barrier((ot, stats))
        *o_parts, kt = call(
            functools.partial(attended_body, cn),
            (quad,) * cn + (sds((nj, D, TK), BF),),
            1,
            2,
            [pltpu.VMEM((nrow, D), BF)],
            pl.CostEstimate(flops=0, bytes_accessed=1 << 22, transcendentals=0),
        )(meta, late_ot, ks)
        o_back = [o_parts[0]] + [share(part, shift, True) for part, shift in zip(o_parts[1:], shifts[1:])]
    kv_near, kv_far, *q_parts = call(
        functools.partial(backward_body, cn, nk),
        (sds((n, BLK, 2 * D), BF),) * 2 + (quad,) * cn,
        1,
        cn + 6,
        [
            pltpu.VMEM((nkey, D), F32),
            pltpu.VMEM((nkey, D), F32),
            pltpu.VMEM((D, ROWS), F32),
            pltpu.VMEM((nrow, D), BF),
            pltpu.VMEM((ROWS, D), BF),
            pltpu.VMEM((1, nrow), F32),
            pltpu.VMEM((1, nrow), F32),
        ],
        pl.CostEstimate(flops=8 * work * D, bytes_accessed=1 << 22, transcendentals=0),
    )(meta, *all_stats, logs, qn, gt, kt, vs, weights)
    with jax.named_scope("keys_out"):
        kv_near, kv_far, q_parts, o_back = lax.optimization_barrier((kv_near, kv_far, q_parts, o_back))
        kv_part = call(add_body, sds((n, BLK, 2 * D), BF), 0, 2)(kv_near, cross(kv_far))
        kv_parts = lax.all_to_all(kv_part, XAXES + ("z",), split_axis=0, concat_axis=0, tiled=True)
    opposite = [(ys - shift) % ys for shift in shifts]
    with jax.named_scope("queries_out"):
        back = [q_parts[0]] + [share(part, shift, True) for part, shift in zip(q_parts[1:], shifts[1:])]
        late_stats = [all_stats[i] for i in opposite]
        kv_part, late_stats = lax.optimization_barrier((kv_part, late_stats))
        attended = call(
            functools.partial(attended_sum_body, cn),
            quad,
            1,
            2 * cn,
            [pltpu.VMEM((nrow, D), F32)],
            pl.CostEstimate(flops=0, bytes_accessed=1 << 22, transcendentals=0),
        )(meta, *late_stats, *o_back)
        sums = call(functools.partial(sum_body, cn), (wide,) * HEADS, 0, cn + 1)(attended, *back)
        final = [sums[0]] + [flip(XAXES, sums[x], x) for x in range(1, HEADS)]
    full, thin = sds(queries.shape, BF), sds(keys.shape, BF)
    return call(place_body, (full, full, thin, thin), 1, HEADS + 1)(head_word, *final, kv_parts)


def solution(mesh):
    heads, outer, inner = (mesh.shape[name] for name in ("head", "outer", "inner"))
    names = ("xhi", "core", "xlo", "z", "inner")
    split = Mesh(mesh.devices.reshape(heads // 2, 2, 2, outer // 2, inner), names)
    rows = P(names, None)
    return jax.shard_map(
        per_device,
        mesh=split,
        in_specs=(rows, rows, rows, rows, P()),
        out_specs=(rows, rows, rows, rows),
        check_vma=False,
    )
```

```python
import functools
import math

import jax
import jax.numpy as jnp
from jax import lax
from jax.experimental import pallas as pl
from jax.experimental.pallas import tpu as pltpu
from jax.sharding import Mesh, PartitionSpec as P

D = 128
BLK = 32
G = 4
HEADS = 4
TB = 4
ROWS = TB * BLK * G
KB = 16
TK = KB * BLK
SUB = 256
SCALE = 1.0 / math.sqrt(D)
C2 = SCALE * math.log2(math.e)
LOW = -1e30
XAXES = ("xhi", "xlo")
LIMIT = 20 * 1024 * 1024
F32, BF = jnp.float32, jnp.bfloat16
VMEM = pl.BlockSpec(memory_space=pltpu.VMEM)
HBM = pl.BlockSpec(memory_space=pltpu.HBM)
SMEM = pl.BlockSpec(memory_space=pltpu.SMEM)


def mo(value, by):
    return pl.multiple_of(value, by)


def call(body, out_shape, n_smem, n_in, scratch=(), cost=None, space=VMEM, limit=LIMIT):
    return pl.pallas_call(
        body,
        out_shape=out_shape,
        in_specs=[SMEM] * n_smem + [space] * n_in,
        out_specs=jax.tree.map(lambda _: VMEM, out_shape),
        scratch_shapes=list(scratch),
        compiler_params=pltpu.CompilerParams(vmem_limit_bytes=limit),
        cost_estimate=cost,
    )


def sds(shape, dtype):
    return jax.ShapeDtypeStruct(shape, dtype)


def pack_body(head, q_in, k_in, v_in, g_in, *refs):
    sends, kv_out = refs[:HEADS], refs[HEADS]
    q, k, v, g, sems = refs[HEADS + 1 :]
    copies = [
        pltpu.make_async_copy(source, target, sems.at[n])
        for n, (source, target) in enumerate(((k_in, k), (v_in, v), (q_in, q), (g_in, g)))
    ]
    for copy in copies:
        copy.start()
    copies[0].wait()
    copies[1].wait()
    fan = kv_out.shape[0] // HEADS
    for j in range(HEADS):
        both = jnp.concatenate([k[:, j * D : (j + 1) * D], v[:, j * D : (j + 1) * D]], axis=1)
        for f in range(fan):
            kv_out[j * fan + f] = both
    h = head[0]
    copies[2].wait()
    copies[3].wait()
    for x in range(HEADS):
        cols = pl.ds(mo((h ^ x) * (G * D), G * D), G * D)
        sends[x][:, : G * D] = q[:, cols]
        sends[x][:, G * D :] = g[:, cols]


def hold_body(rows, out):
    out[...] = rows[...]


def collect_body(*refs):
    parts, (queries, grads) = refs[:HEADS], refs[HEADS:]
    for x in range(HEADS):
        queries[x] = parts[x][:, : G * D]
        grads[x] = parts[x][:, G * D :]


def tiles_needed(meta, nq, nk, t, kb):
    last = meta[nq + nk + t * TB + TB - 1]
    need = jnp.int32(0)
    for j in range(nk // kb):
        need += (meta[2 * nq + nk + j * kb] <= last).astype(jnp.int32)
    return need


def in_pairs(need, step, width, state):
    state = lax.fori_loop(0, need // 2, functools.partial(step, 2 * width), state)
    return lax.fori_loop(need // 2 * 2, need, functools.partial(step, width), state)


def query_lane(meta, nq, nk, t):
    lane = lax.broadcasted_iota(jnp.int32, (1, ROWS), 1)
    block = (lane // BLK) % TB
    pos = jnp.zeros((1, ROWS), jnp.int32)
    for b in range(TB):
        pos = jnp.where(block == b, meta[nq + nk + t * TB + b], pos)
    return pos * BLK + lane % BLK


def masked_scores(meta, nq, nk, scores, lane_pos, first):
    row = lax.broadcasted_iota(jnp.int32, (BLK, ROWS), 0)
    parts = []
    for b in range(scores.shape[0] // BLK):
        at = meta[2 * nq + nk + first + b] * BLK
        allowed = row <= lane_pos - at
        parts.append(jnp.where(allowed, scores[b * BLK : (b + 1) * BLK], LOW))
    return jnp.concatenate(parts, axis=0)


def dot(a, b):
    return lax.dot_general(a, b, (((1,), (0,)), ((), ())), preferred_element_type=F32)


def row_slots(meta, cn):
    for r in range(cn):
        for x in range(HEADS):
            n = meta[r * HEADS + x]
            yield r, x, (n // TB) * ROWS + (n % TB) * BLK


def rows_at(base, g):
    return pl.ds(mo(base + g * TB * BLK, BLK), BLK)


def stage_body(cn, meta, *refs):
    parts, (rows, tiles) = refs[:cn], refs[cn:]
    for r, x, base in row_slots(meta, cn):
        for g in range(G):
            rows[rows_at(base, g), :] = parts[r][x, :, g * D : (g + 1) * D]
    for t in range(tiles.shape[0]):
        tiles[t] = rows[t * ROWS : (t + 1) * ROWS, :].T


def stage_keys_body(nq, nk, meta, kv_near, kv_far, ks, vs, vt):
    for s in range(nk):
        at = pl.ds(mo(meta[nq + s] * BLK, BLK), BLK)
        kv = (kv_near, kv_far)[s // (nk // 2)]
        ks[at, :] = kv[s % (nk // 2), :, :D]
        vs[at, :] = kv[s % (nk // 2), :, D:]
    for j in range(vt.shape[0]):
        vt[j] = vs[j * TK : (j + 1) * TK, :].T


def stage_all_body(cn, nk, meta, *refs):
    parts, (kv_near, kv_far), outs = refs[:cn], refs[cn : cn + 2], refs[cn + 2 :]
    stage_keys_body(cn * HEADS, nk, meta, kv_near, kv_far, *outs[2:])
    stage_body(cn, meta, *parts, *outs[:2])


def forward_body(nq, nk, meta, qt, ks, vt, logs, ot, weights_out, sbuf):
    def tile(t, unused):
        need = tiles_needed(meta, nq, nk, t, KB)
        lane_pos = query_lane(meta, nq, nk, t)
        query = qt[t]

        def score(width, j, run):
            for c in range(0, width, SUB):
                at = pl.ds(mo(j * width + c, SUB), SUB)
                scores = dot(ks[at, :], query)
                scores = masked_scores(meta, nq, nk, scores, lane_pos, (j * width + c) // BLK)
                sbuf[at, :] = scores
                run = jnp.maximum(run, jnp.max(scores, axis=0, keepdims=True))
            return run

        top = in_pairs(need, score, TK, jnp.full((1, ROWS), LOW * 0.1, F32)) * C2

        def step(width, j, state):
            total, acc = state
            for c in range(0, width, SUB):
                at = pl.ds(mo(j * width + c, SUB), SUB)
                weights = jnp.exp2(sbuf[at, :] * C2 - top)
                total += jnp.sum(weights, axis=0, keepdims=True)
                rounded = weights.astype(BF)
                weights_out[t, at, :] = rounded
                acc += dot(vt[j * (width // TK) + c // TK, :, c % TK : c % TK + SUB], rounded)
            return total, acc

        state = (jnp.zeros((1, ROWS), F32), jnp.zeros((D, ROWS), F32))
        total, acc = in_pairs(need, step, TK, state)
        some = total > 0.0
        safe = jnp.where(some, total, 1.0)
        lanes = pl.ds(mo(t * ROWS, ROWS), ROWS)
        logs[0:1, lanes] = jnp.where(some, top + jnp.log2(safe), LOW)
        logs[1:2, lanes] = top
        ot[t] = acc * jnp.where(some, 1.0 / safe, 0.0)
        return unused

    lax.fori_loop(0, nq // TB, tile, 0)


def delta_body(cn, meta, logs, ot, *refs):
    parts, (stats, gt, gn) = refs[:cn], refs[cn:]
    for r, x, base in row_slots(meta, cn):
        for g in range(G):
            gn[rows_at(base, g), :] = parts[r][x, :, g * D : (g + 1) * D]
    stats[0:1, :] = logs[0:1, :]
    for t in range(gt.shape[0]):
        lanes = slice(t * ROWS, (t + 1) * ROWS)
        grads = gn[lanes, :].T
        gt[t] = grads
        stats[1:2, lanes] = jnp.sum(ot[t] * grads.astype(F32), axis=0, keepdims=True)


def attended_body(cn, meta, ot, ks, *refs):
    outs, kt, on = refs[:cn], refs[cn], refs[cn + 1]
    for t in range(ot.shape[0]):
        on[t * ROWS : (t + 1) * ROWS, :] = ot[t].astype(BF).T
    for r, x, base in row_slots(meta, cn):
        for g in range(G):
            outs[r][x, :, g * D : (g + 1) * D] = on[rows_at(base, g), :]
    for j in range(kt.shape[0]):
        kt[j] = ks[j * TK : (j + 1) * TK, :].T


def combine(stats):
    logs = [s[0:1, :] for s in stats]
    top = functools.reduce(jnp.maximum, logs)
    parts = [jnp.exp2(log - top) for log in logs]
    whole = functools.reduce(jnp.add, parts)
    return parts, whole, top


def backward_body(cn, nk, meta, *refs):
    stats = refs[:cn]
    logs, qn, gt, kt, vs, weights = refs[cn : cn + 6]
    near, far, *outs = refs[cn + 6 : 2 * cn + 8]
    dk, dv, dqt, dqn, gn, scale_all, delta_all = refs[2 * cn + 8 :]
    nq = cn * HEADS
    nt = nq // TB

    parts, whole, top = combine(stats)
    scale_all[...] = jnp.exp2(logs[1:2, :] - top) / whole
    delta_all[...] = functools.reduce(jnp.add, [p * s[1:2, :] for p, s in zip(parts, stats)]) / whole
    dk[...] = jnp.zeros_like(dk)
    dv[...] = jnp.zeros_like(dv)

    def tile(t, unused):
        need = tiles_needed(meta, nq, nk, t, SUB // BLK)
        lanes = pl.ds(mo(t * ROWS, ROWS), ROWS)
        scale, delta = scale_all[:, lanes], delta_all[:, lanes]
        gn[...] = (gt[t].astype(F32) * scale).astype(BF).T
        dqt[...] = jnp.zeros_like(dqt)

        def step(width, j, state):
            for c in range(0, width, SUB):
                keys = pl.ds(mo(j * width + c, SUB), SUB)
                own = weights[t, keys, :]
                lean = (dot(vs[keys, :], gt[t]) - delta) * scale
                grad_scores = (own.astype(F32) * lean).astype(BF)
                dv[keys, :] += dot(own, gn[...])
                dk[keys, :] += dot(grad_scores, qn[lanes, :])
                dqt[...] += dot(kt[j * width // TK, :, c : c + SUB], grad_scores)
            return state

        in_pairs(need, step, SUB, 0)
        dqn[lanes, :] = (dqt[...] * SCALE).astype(BF).T
        return unused

    lax.fori_loop(0, nt, tile, 0)
    for s in range(nk):
        at = pl.ds(mo(meta[nq + s] * BLK, BLK), BLK)
        kv_out = (near, far)[s // (nk // 2)]
        kv_out[s % (nk // 2), :, :D] = (dk[at, :] * SCALE).astype(BF)
        kv_out[s % (nk // 2), :, D:] = dv[at, :].astype(BF)
    for r, x, base in row_slots(meta, cn):
        for g in range(G):
            outs[r][x, :, g * D : (g + 1) * D] = dqn[rows_at(base, g), :]


def add_body(one, two, out):
    out[...] = (one[...].astype(F32) + two[...].astype(F32)).astype(BF)


def attended_sum_body(cn, meta, *refs):
    stats, attended, out, columns = refs[:cn], refs[cn : 2 * cn], refs[2 * cn], refs[2 * cn + 1]
    parts, whole, top = combine(stats)
    inverse = 1.0 / whole
    spread = D // cn
    tall = jnp.concatenate([jnp.broadcast_to(p * inverse, (spread, p.shape[1])) for p in parts], axis=0)
    for t in range(tall.shape[1] // ROWS):
        columns[t * ROWS : (t + 1) * ROWS, :] = tall[:, t * ROWS : (t + 1) * ROWS].T
    for r, x, base in row_slots(meta, 1):
        for g in range(G):
            cols = slice(g * D, (g + 1) * D)
            column = columns[rows_at(base, g), :]
            total = jnp.zeros((BLK, D), F32)
            for i in range(cn):
                total += column[:, i * spread : i * spread + 1] * attended[i][x, :, cols].astype(F32)
            out[x, :, cols] = total.astype(BF)


def sum_body(cn, attended, *refs):
    grads, outs = refs[:cn], refs[cn:]
    for x in range(HEADS):
        outs[x][:, : G * D] = attended[x]
        total = grads[0][x].astype(F32)
        for i in range(1, cn):
            total += grads[i][x].astype(F32)
        outs[x][:, G * D :] = total.astype(BF)


def place_body(head, *refs):
    parts, shares = refs[:HEADS], refs[HEADS]
    attended, grad, dk, dv = refs[HEADS + 1 :]
    h = head[0]
    for x in range(HEADS):
        cols = pl.ds(mo((h ^ x) * (G * D), G * D), G * D)
        attended[:, cols] = parts[x][:, : G * D]
        grad[:, cols] = parts[x][:, G * D :]
    fan = shares.shape[0] // HEADS
    for j in range(HEADS):
        total = shares[j * fan].astype(F32)
        for f in range(1, fan):
            total += shares[j * fan + f].astype(F32)
        dk[:, j * D : (j + 1) * D] = total[:, :D].astype(BF)
        dv[:, j * D : (j + 1) * D] = total[:, D:].astype(BF)


def flip(axis, value, x):
    return lax.ppermute(value, axis, [(j, j ^ x) for j in range(HEADS)])


def per_device(queries, keys, values, grad_out, block_order):
    xs, zs, ys = lax.axis_size("xlo"), lax.axis_size("z"), lax.axis_size("inner")
    head, core = lax.axis_index(XAXES), lax.axis_index("core")
    z, inner = lax.axis_index("z"), lax.axis_index("inner")
    shifts = range(ys)
    cn = ys
    nq = cn * HEADS
    n = HEADS * zs
    nk = 2 * n

    def share(value, shift, back=False):
        step = ys - shift if back else shift
        return lax.ppermute(value, "inner", [(j, (j + step) % ys) for j in range(ys)])

    def cross(value):
        return lax.ppermute(value, "core", [(0, 1), (1, 0)])

    def block_of(x, c, j, k):
        return (((x // xs * 2 + c) * xs + x % xs) * zs + j) * ys + k

    slot = jnp.arange(nq, dtype=jnp.int32)
    q_block = block_of(head ^ (slot % HEADS), core, z, (inner - slot // HEADS) % ys)
    slot = jnp.arange(nk, dtype=jnp.int32)
    k_block = block_of((slot % n) // zs, core ^ (slot // n), slot % zs, inner)
    every = jnp.arange(block_order.shape[0], dtype=jnp.int32)

    def ranked(block):
        pos = jnp.sum(jnp.where(block[:, None] == every[None, :], block_order[None, :], 0), axis=1)
        rank = jnp.sum((pos[None, :] < pos[:, None]).astype(jnp.int32), axis=1)
        n = block.shape[0]
        hit = rank[None, :] == jnp.arange(n, dtype=jnp.int32)[:, None]
        return rank, jnp.sum(jnp.where(hit, pos[None, :], 0), axis=1)

    q_rank, q_sorted = ranked(q_block)
    k_rank, k_sorted = ranked(k_block)
    meta = jnp.concatenate([q_rank, k_rank, q_sorted, k_sorted])
    head_word = head[None].astype(jnp.int32)

    wide, quad = sds((BLK, 2 * G * D), BF), sds((HEADS, BLK, G * D), BF)
    full_in, thin_in = pltpu.VMEM(queries.shape, BF), pltpu.VMEM(keys.shape, BF)
    *sends, kv_send = call(
        pack_body,
        (wide,) * HEADS + (sds((n, BLK, 2 * D), BF),),
        1,
        4,
        [full_in, thin_in, thin_in, full_in, pltpu.SemaphoreType.DMA((4,))],
        space=HBM,
        limit=60 * 1024 * 1024,
    )(head_word, queries, keys, values, grad_out)
    with jax.named_scope("keys_in"):
        kv = lax.all_to_all(kv_send, XAXES + ("z",), split_axis=0, concat_axis=0, tiled=True)

    def spread(mine):
        return [mine] + [share(mine, shift) for shift in shifts[1:]]

    nrow, nkey = nq * BLK * G, nk * BLK
    nt, nj = nq // TB, nk // KB
    tiles = sds((nt, D, ROWS), BF)
    rows = sds((nrow, D), BF)
    key_rows = sds((nkey, D), BF)
    pairs = sds((nt, nkey, ROWS), BF)
    stat = sds((2, nrow), F32)
    work = nrow * nkey
    with jax.named_scope("queries_in"):
        held = call(hold_body, wide, 0, 1)(sends[0])
        arrived = [held] + [flip(XAXES, sends[x], x) for x in range(1, HEADS)]
        arrived, meta = lax.optimization_barrier((arrived, meta))
        q_mine, g_mine = call(collect_body, (quad, quad), 0, HEADS)(*arrived)
        q_all = spread(q_mine)
    with jax.named_scope("keys_cross_in"):
        q_all, g_mine, kv = lax.optimization_barrier((q_all, g_mine, kv))
        qn, qt, ks, vs, vt = call(
            functools.partial(stage_all_body, cn, nk),
            (rows, tiles, key_rows, key_rows, sds((nj, D, TK), BF)),
            1,
            cn + 2,
        )(meta, *q_all, kv, cross(kv))
    with jax.named_scope("grads_in"):
        g_all = spread(g_mine)
    logs, ot, weights = call(
        functools.partial(forward_body, nq, nk),
        (stat, sds((nt, D, ROWS), F32), pairs),
        1,
        3,
        [pltpu.VMEM((nkey, ROWS), F32)],
        pl.CostEstimate(flops=4 * work * D, bytes_accessed=1 << 22, transcendentals=work),
    )(meta, qt, ks, vt)
    stats, gt = call(
        functools.partial(delta_body, cn), (stat, tiles), 1, cn + 2, [pltpu.VMEM((nrow, D), BF)]
    )(meta, logs, ot, *g_all)
    with jax.named_scope("stats"):
        all_stats = [stats] + [share(stats, shift) for shift in shifts[1:]]
    with jax.named_scope("attended_out"):
        late_ot, _ = lax.optimization_barrier((ot, stats))
        *o_parts, kt = call(
            functools.partial(attended_body, cn),
            (quad,) * cn + (sds((nj, D, TK), BF),),
            1,
            2,
            [pltpu.VMEM((nrow, D), BF)],
            pl.CostEstimate(flops=0, bytes_accessed=1 << 22, transcendentals=0),
        )(meta, late_ot, ks)
        o_back = [o_parts[0]] + [share(part, shift, True) for part, shift in zip(o_parts[1:], shifts[1:])]
    kv_near, kv_far, *q_parts = call(
        functools.partial(backward_body, cn, nk),
        (sds((n, BLK, 2 * D), BF),) * 2 + (quad,) * cn,
        1,
        cn + 6,
        [
            pltpu.VMEM((nkey, D), F32),
            pltpu.VMEM((nkey, D), F32),
            pltpu.VMEM((D, ROWS), F32),
            pltpu.VMEM((nrow, D), BF),
            pltpu.VMEM((ROWS, D), BF),
            pltpu.VMEM((1, nrow), F32),
            pltpu.VMEM((1, nrow), F32),
        ],
        pl.CostEstimate(flops=8 * work * D, bytes_accessed=1 << 22, transcendentals=0),
    )(meta, *all_stats, logs, qn, gt, kt, vs, weights)
    with jax.named_scope("keys_out"):
        kv_near, kv_far, q_parts, o_back = lax.optimization_barrier((kv_near, kv_far, q_parts, o_back))
        kv_part = call(add_body, sds((n, BLK, 2 * D), BF), 0, 2)(kv_near, cross(kv_far))
        kv_parts = lax.all_to_all(kv_part, XAXES + ("z",), split_axis=0, concat_axis=0, tiled=True)
    opposite = [(ys - shift) % ys for shift in shifts]
    with jax.named_scope("queries_out"):
        back = [q_parts[0]] + [share(part, shift, True) for part, shift in zip(q_parts[1:], shifts[1:])]
        late_stats = [all_stats[i] for i in opposite]
        kv_part, late_stats = lax.optimization_barrier((kv_part, late_stats))
        attended = call(
            functools.partial(attended_sum_body, cn),
            quad,
            1,
            2 * cn,
            [pltpu.VMEM((nrow, D), F32)],
            pl.CostEstimate(flops=0, bytes_accessed=1 << 22, transcendentals=0),
        )(meta, *late_stats, *o_back)
        sums = call(functools.partial(sum_body, cn), (wide,) * HEADS, 0, cn + 1)(attended, *back)
        final = [sums[0]] + [flip(XAXES, sums[x], x) for x in range(1, HEADS)]
    full, thin = sds(queries.shape, BF), sds(keys.shape, BF)
    return call(place_body, (full, full, thin, thin), 1, HEADS + 1)(head_word, *final, kv_parts)


def solution(mesh):
    heads, outer, inner = (mesh.shape[name] for name in ("head", "outer", "inner"))
    names = ("xhi", "core", "xlo", "z", "inner")
    split = Mesh(mesh.devices.reshape(heads // 2, 2, 2, outer // 2, inner), names)
    rows = P(names, None)
    return jax.shard_map(
        per_device,
        mesh=split,
        in_specs=(rows, rows, rows, rows, P()),
        out_specs=(rows, rows, rows, rows),
        check_vma=False,
    )
```
